512 devices in a mesh: row: 16 (over z), col: 32 (over x, y, core).
Axes of the slice: x: 4, y: 4, z: 16, core: 2. Of those that a mesh axis runs over, the one named last changes fastest.
Arguments:
- noise: bfloat16 [8192, 4096], P('row', 'col'), may hold values from -6 to 6
- data: bfloat16 [16384, 4096], P('col', 'row'), may hold values from -6 to 6
Outputs:
- target: bfloat16 [8192, 4096], P('row', 'col')
- noise_potential: float32 [8192], P('row')
- data_potential: float32 [16384], P('col')
The draws below stay inside these ranges and needn't reach their ends.
All inputs are finite; a program needn't handle non-finite values.
Results may differ from the reference program's by a relative error of at most 0.015.
Values may be sent and summed in bfloat16 or wider, within the bound.
No kernel may reach another device: no remote copies, remote signals or barrier semaphores. Data moves between devices by JAX's collectives and lax.ppermute only.
A program may use at most 64 MiB of HBM per device.

```python
import math
import jax
import jax.numpy as jnp
from jax import lax

D = 4096
DATA_DEV = 512
ITERS = 4
N = 8192
M = 16384
N_COL = 32


def level_of(key, shape, split, least, top_value):
    level = 1.0
    for dim, shards_of in split:
        draws = jax.random.uniform(jax.random.fold_in(jax.random.fold_in(key, 6), dim), (shards_of,), jnp.float32, least / len(split), top_value / len(split))
        level = level * jnp.repeat(jnp.exp(draws), shape[dim] // shards_of).reshape((-1,) + (1,) * (len(shape) - 1 - dim))
    return level


def gaussian(own_key, shape, width, limit, split=(), held_as=jnp.bfloat16):
    loudness = level_of(own_key, shape, split, -0.22, 0.18) if split else 1.0
    drawn = jax.random.normal(own_key, shape, jnp.float32) * width * loudness
    return jnp.minimum(jnp.maximum(drawn, -limit), limit).astype(held_as)


def setup_inputs(seed: int = 0) -> dict:
    key_list = jax.random.split(jax.random.key(seed), 3)
    noise = gaussian(key_list[0], (N, D), 1.0, 6.0, ((0, 16), (1, 32)))
    data = gaussian(key_list[1], (M, D), 1.0, 6.0, ((0, 32), (1, 16)))
    return dict(noise=noise, data=data)


blur = 0.01


def reference(noise, data):
    noise_f = noise.astype(jnp.float32)
    data_f = data.astype(jnp.float32)
    xsq = jnp.sum(noise_f * noise_f, axis=1)
    ysq = jnp.sum(data_f * data_f, axis=1)
    inner = jnp.dot(noise_f, data_f.T, preferred_element_type=jnp.float32)
    cost = (xsq[:, None] + ysq[None, :] - 2.0 * inner) / D
    data_potential = jnp.zeros((M,), jnp.float32)
    noise_potential = jnp.zeros((N,), jnp.float32)
    for step in range(ITERS):
        noise_potential = -blur * jax.nn.logsumexp((data_potential[None, :] - cost) / blur, axis=1)
        data_potential = blur * math.log(N / M) - blur * jax.nn.logsumexp((noise_potential[:, None] - cost) / blur, axis=0)
    plan = jnp.exp((noise_potential[:, None] + data_potential[None, :] - cost) / blur)
    mass = jnp.sum(plan, axis=1)
    weights = plan.astype(jnp.bfloat16)

    def add_block(index, total):
        start = (index * DATA_DEV).astype(jnp.int32)
        cols = lax.dynamic_slice_in_dim(weights, start, DATA_DEV, 1).astype(jnp.float32)
        rows = lax.dynamic_slice_in_dim(data, start, DATA_DEV, 0).astype(jnp.float32)
        part = jnp.dot(cols, rows, preferred_element_type=jnp.float32).astype(jnp.bfloat16)
        return total + part.astype(jnp.float32)

    numerator = lax.fori_loop(jnp.int32(0), jnp.int32(N_COL), add_block, jnp.zeros((N, D), jnp.float32))
    target = (numerator / mass[:, None] - noise_f).astype(jnp.bfloat16)
    return target, noise_potential, data_potential
```

```python
import functools
import math

import jax
import jax.numpy as jnp
from jax import lax
from jax.experimental import pallas as pl
from jax.experimental.pallas import tpu as pltpu
from jax.sharding import PartitionSpec as P

ITERS = 4
blur = 0.01
X, Y, CORES = 4, 4, 2
CHIPS = X * Y
EXTRA = 16


def place(x, y, core):
    return (x * Y + y) * CORES + core


PLANE = [[place(x, y, core) for x in range(X) for y in range(Y)] for core in range(CORES)]
SWAP = [(index, index ^ 1) for index in range(CHIPS * CORES)]


def gathered(value, axis, count):
    copies = jnp.broadcast_to(value[None], (count,) + value.shape)
    return lax.all_to_all(copies, axis, 0, 0)


def cost_kernel(core_ref, own_ref, other_ref, data_ref, xsq_ref, ysq_ref, out_ref, *, scale):
    step = pl.program_id(0)
    first = core_ref[0] == 0
    own = own_ref[0]
    other = other_ref[0]
    rows = jnp.concatenate([jnp.where(first, own, other), jnp.where(first, other, own)], axis=1)
    part = lax.dot_general(
        rows, data_ref[0], (((1,), (1,)), ((), ())), preferred_element_type=jnp.float32
    )

    @pl.when(step == 0)
    def _():
        out_ref[...] = part

    @pl.when(step > 0)
    def _():
        out_ref[...] += part

    @pl.when(step == pl.num_programs(0) - 1)
    def _():
        out_ref[...] = (2.0 * out_ref[...] - xsq_ref[...] - ysq_ref[...]) * scale


def scores_of(core, own, other, chunks, xsq, ysq, scale):
    steps, rows, half = own.shape
    columns, width = chunks.shape[1:]
    return pl.pallas_call(
        functools.partial(cost_kernel, scale=scale),
        grid_spec=pltpu.PrefetchScalarGridSpec(
            num_scalar_prefetch=1,
            grid=(steps,),
            in_specs=[
                pl.BlockSpec((1, rows, half), lambda k, core: (k, 0, 0)),
                pl.BlockSpec((1, rows, half), lambda k, core: (k, 0, 0)),
                pl.BlockSpec((1, columns, width), lambda k, core: (k, 0, 0)),
                pl.BlockSpec((rows, 1), lambda k, core: (0, 0)),
                pl.BlockSpec((1, columns), lambda k, core: (0, 0)),
            ],
            out_specs=pl.BlockSpec((rows, columns), lambda k, core: (0, 0)),
        ),
        out_shape=jax.ShapeDtypeStruct((rows, columns), jnp.float32),
        compiler_params=pltpu.CompilerParams(
            dimension_semantics=("arbitrary",), vmem_limit_bytes=32 * 1024 * 1024
        ),
        name="cost",
    )(core, own, other, chunks, xsq[:, None], ysq[None, :])


def mix_kernel(core_ref, own_w_ref, other_w_ref, own_d_ref, other_d_ref, out_ref):
    rows = own_w_ref.shape[0]
    count, _, half = own_d_ref.shape
    own_d = jnp.concatenate([own_d_ref[k] for k in range(count)], axis=1)
    other_d = jnp.concatenate([other_d_ref[k] for k in range(count)], axis=1)
    own_w = own_w_ref[...]
    other_w = other_w_ref[...]
    total = jnp.dot(own_w, own_d, preferred_element_type=jnp.float32)
    total += jnp.dot(other_w, other_d, preferred_element_type=jnp.float32)
    ones = jnp.ones((EXTRA, own_w.shape[1]), jnp.bfloat16)
    contract = (((1,), (1,)), ((), ()))
    left = lax.dot_general(ones, own_w, contract, preferred_element_type=jnp.float32)
    left += lax.dot_general(ones, other_w, contract, preferred_element_type=jnp.float32)
    line = lax.broadcasted_iota(jnp.int32, (EXTRA, half), 0)
    tail = jnp.zeros((EXTRA, half), jnp.float32)
    pieces = rows // half
    for part in range(3):
        rounded = left.astype(jnp.bfloat16).astype(jnp.float32)
        left = left - rounded
        for k in range(pieces):
            tail = jnp.where(line == part * pieces + k, rounded[:, k * half : (k + 1) * half], tail)
    for k in range(count):
        out_ref[k, :rows, :] = total[:, k * half : (k + 1) * half].astype(jnp.bfloat16)
        out_ref[k, rows:, :] = tail.astype(jnp.bfloat16)


def mixed(core, own_w, other_w, chunks, other_d):
    steps, columns, half = other_d.shape
    rows = own_w.shape[0]
    count = 2
    return pl.pallas_call(
        mix_kernel,
        grid_spec=pltpu.PrefetchScalarGridSpec(
            num_scalar_prefetch=1,
            grid=(steps // count,),
            in_specs=[
                pl.BlockSpec((rows, columns), lambda k, core: (0, 0)),
                pl.BlockSpec((rows, columns), lambda k, core: (0, 0)),
                pl.BlockSpec((count, columns, half), lambda k, core: (k, 0, core[0])),
                pl.BlockSpec((count, columns, half), lambda k, core: (k, 0, 0)),
            ],
            out_specs=pl.BlockSpec((count, rows + EXTRA, half), lambda k, core: (k, 0, 0)),
        ),
        out_shape=jax.ShapeDtypeStruct((steps, rows + EXTRA, half), jnp.bfloat16),
        compiler_params=pltpu.CompilerParams(
            dimension_semantics=("arbitrary",), vmem_limit_bytes=32 * 1024 * 1024
        ),
        name="mix",
    )(core, own_w, other_w, chunks, other_d)


def shards(noise, data):
    n_row, n_col = lax.axis_size("row"), lax.axis_size("col")
    rows, half = noise.shape
    columns = data.shape[0]
    width = half * n_col
    core = lax.rem(lax.axis_index("col"), CORES)
    core_word = jnp.full((1,), core, jnp.int32)

    chunks = lax.all_gather(data, "row")
    own = lax.all_to_all(
        jnp.broadcast_to(noise[None], (CHIPS,) + noise.shape), "col", 0, 0, axis_index_groups=PLANE
    )
    other = lax.ppermute(own, "col", SWAP)
    wide = noise.astype(jnp.float32)
    xsq = jnp.sum(gathered(jnp.sum(wide * wide, axis=1)[None], "col", n_col), axis=(0, 1))
    data_wide = data.astype(jnp.float32)
    ysq = jnp.sum(gathered(jnp.sum(data_wide * data_wide, axis=1)[None], "row", n_row), axis=(0, 1))

    scores = scores_of(core_word, own, other, chunks, xsq, ysq, 1.0 / (width * blur))
    sent = jnp.where(core == 0, chunks[:, :, half:], chunks[:, :, :half])
    other_d = lax.ppermute(sent, "col", SWAP)

    shift = math.log(rows * n_row / (columns * n_col))
    f = g = None
    for step in range(ITERS):
        if step == 0:
            top = jnp.max(scores, axis=1)
            total = jnp.sum(jnp.exp(scores - top[:, None]), axis=1)
            pairs = gathered(jnp.stack([top, total]), "col", n_col)
            top = jnp.max(pairs[:, 0], axis=0)
            f = -top - jnp.log(jnp.sum(pairs[:, 1] * jnp.exp(pairs[:, 0] - top), axis=0))
            shifted = scores + f[:, None]
            top = jnp.max(shifted, axis=0)
            total = jnp.sum(jnp.exp(shifted - top[None, :]), axis=0)
            pairs = gathered(jnp.stack([top, total]), "row", n_row)
            top = jnp.max(pairs[:, 0], axis=0)
            g = shift - top - jnp.log(jnp.sum(pairs[:, 1] * jnp.exp(pairs[:, 0] - top), axis=0))
        else:
            total = jnp.sum(jnp.exp(scores + f[:, None] + g[None, :]), axis=1)
            f = f - jnp.log(jnp.sum(gathered(total[None], "col", n_col), axis=(0, 1)))
            total = jnp.sum(jnp.exp(scores + f[:, None] + g[None, :]), axis=0)
            g = g + shift - jnp.log(jnp.sum(gathered(total[None], "row", n_row), axis=(0, 1)))

    own_w = jnp.exp(scores + f[:, None] + g[None, :]).astype(jnp.bfloat16)
    other_w = lax.ppermute(own_w, "col", SWAP)
    pieces = mixed(core_word, own_w, other_w, chunks, other_d)
    landed = lax.all_to_all(pieces, "col", 0, 0, axis_index_groups=PLANE)
    summed = jnp.sum(landed.astype(jnp.float32), axis=0)
    mass = jnp.sum(summed[rows:].reshape(-1)[: 3 * rows].reshape(3, rows), axis=0)
    target = (summed[:rows] / mass[:, None] - wide).astype(jnp.bfloat16)
    return (target, f * blur, g * blur)


def solution(mesh):
    return jax.shard_map(
        shards,
        mesh=mesh,
        in_specs=(P("row", "col"), P("col", "row")),
        out_specs=(P("row", "col"), P("row"), P("col")),
        check_vma=False,
    )
```

```python
import functools
import math

import jax
import jax.numpy as jnp
from jax import lax
from jax.experimental import pallas as pl
from jax.experimental.pallas import tpu as pltpu
from jax.sharding import PartitionSpec as P

ITERS = 4
blur = 0.01
X, Y, CORES, Z = 4, 4, 2, 16
CHIPS = X * Y
COLS = CHIPS * CORES
EXTRA = 16
STEP = 4
AXES = ("row", "col")

ORDER = [0]
for far in range(1, Z // 2):
    ORDER += [Z - far, far]
ORDER.append(Z // 2)

PLANE = [
    [z * COLS + (z + k) % CHIPS * CORES + core for k in ORDER] for z in range(Z) for core in range(CORES)
]
SWAP = [(index, index ^ 1) for index in range(COLS)]
FORTH = [(z, (z + 1) % Z) for z in range(Z)]
BACK = [(z, (z - 1) % Z) for z in range(Z)]
LAST = (((1,), (1,)), ((), ()))


def gathered(value, axis, count):
    copies = jnp.broadcast_to(value[None], (count,) + value.shape)
    return lax.all_to_all(copies, axis, 0, 0)


def squares(wide):
    wide = wide.astype(jnp.float32)
    wide = wide * wide
    high = wide.astype(jnp.bfloat16)
    return high, (wide - high.astype(jnp.float32)).astype(jnp.bfloat16)


def cost_kernel(core_ref, noise_ref, *refs, first, scale):
    data_refs, refs = refs[:STEP], refs[STEP:]
    if not first:
        acc_ref, refs = refs[0], refs[3:]
    out_ref, keep_ref, sent_ref = refs
    low = core_ref[0] == 0
    half = noise_ref.shape[2] // CORES
    rows, columns = [], []
    for k in range(STEP):
        rows.append(noise_ref[k])
        chunk = data_refs[k][...]
        columns.append(chunk)
        left, right = chunk[:, :half], chunk[:, half:]
        keep_ref[k] = jnp.where(low, left, right)
        sent_ref[k] = jnp.where(low, right, left)
    rows = jnp.concatenate(rows, axis=1)
    columns = jnp.concatenate(columns, axis=1)
    inner = lax.dot_general(rows, columns, LAST, preferred_element_type=jnp.float32)
    width = rows.shape[1]
    ones = jnp.ones((8, width), jnp.bfloat16)
    wall = jnp.ones((width, 128), jnp.bfloat16)
    high, rest = squares(columns)
    ysq = lax.dot_general(ones, high, LAST, preferred_element_type=jnp.float32)
    ysq += lax.dot_general(ones, rest, LAST, preferred_element_type=jnp.float32)
    high, rest = squares(rows)
    xsq = jnp.dot(high, wall, preferred_element_type=jnp.float32)
    xsq += jnp.dot(rest, wall, preferred_element_type=jnp.float32)
    part = (2.0 * inner - xsq[:, :1] - ysq[:1, :]) * scale
    out_ref[...] = part if first else acc_ref[...] + part


def cost_step(core, latents, chunks, call, carry, scale):
    total, rows, _ = latents.shape
    columns, width = chunks[0].shape
    half = width // CORES
    first = carry is None
    part = pl.BlockSpec((STEP, rows, width), lambda i, core: (call, 0, 0))
    part_d = pl.BlockSpec((STEP, columns, half), lambda i, core: (call, 0, 0))
    tile = pl.BlockSpec((rows, columns), lambda i, core: (0, 0))
    whole = pl.BlockSpec(memory_space=pl.ANY)
    in_specs = [part] + [pl.BlockSpec((columns, width), lambda i, core: (0, 0))] * STEP
    args = [core, latents, *chunks]
    aliases = {}
    if not first:
        aliases = {len(args) + k: k for k in range(3)}
        in_specs += [tile, whole, whole]
        args += list(carry)
    halves = jax.ShapeDtypeStruct((total, columns, half), jnp.bfloat16)
    return pl.pallas_call(
        functools.partial(cost_kernel, first=first, scale=scale),
        grid_spec=pltpu.PrefetchScalarGridSpec(
            num_scalar_prefetch=1, grid=(1,), in_specs=in_specs, out_specs=[tile, part_d, part_d]
        ),
        out_shape=[jax.ShapeDtypeStruct((rows, columns), jnp.float32), halves, halves],
        input_output_aliases=aliases,
        compiler_params=pltpu.CompilerParams(
            dimension_semantics=("arbitrary",), vmem_limit_bytes=48 * 1024 * 1024
        ),
        cost_estimate=pl.CostEstimate(
            flops=2 * rows * columns * width * STEP, bytes_accessed=6 * 1024 * 1024, transcendentals=0
        ),
        name="cost",
    )(*args)


def mix_kernel(own_w_ref, other_w_ref, own_d_ref, other_d_ref, out_ref):
    rows = own_w_ref.shape[0]
    count, _, half = own_d_ref.shape
    own_d = jnp.concatenate([own_d_ref[k] for k in range(count)], axis=1)
    other_d = jnp.concatenate([other_d_ref[k] for k in range(count)], axis=1)
    own_w = own_w_ref[...]
    other_w = other_w_ref[...]
    total = jnp.dot(own_w, own_d, preferred_element_type=jnp.float32)
    total += jnp.dot(other_w, other_d, preferred_element_type=jnp.float32)
    ones = jnp.ones((EXTRA, own_w.shape[1]), jnp.bfloat16)
    left = lax.dot_general(ones, own_w, LAST, preferred_element_type=jnp.float32)
    left += lax.dot_general(ones, other_w, LAST, preferred_element_type=jnp.float32)
    line = lax.broadcasted_iota(jnp.int32, (EXTRA, half), 0)
    tail = jnp.zeros((EXTRA, half), jnp.float32)
    pieces = rows // half
    for part in range(3):
        rounded = left.astype(jnp.bfloat16).astype(jnp.float32)
        left = left - rounded
        for k in range(pieces):
            tail = jnp.where(line == part * pieces + k, rounded[:, k * half : (k + 1) * half], tail)
    for k in range(count):
        out_ref[k, :rows, :] = total[:, k * half : (k + 1) * half].astype(jnp.bfloat16)
        out_ref[k, rows:, :] = tail.astype(jnp.bfloat16)


def mixed(own_w, other_w, own_d, other_d):
    steps, columns, half = other_d.shape
    rows = own_w.shape[0]
    count = 2
    weights = pl.BlockSpec((rows, columns), lambda k: (0, 0))
    pair = pl.BlockSpec((count, columns, half), lambda k: (k, 0, 0))
    return pl.pallas_call(
        mix_kernel,
        grid=(steps // count,),
        in_specs=[weights, weights, pair, pair],
        out_specs=pl.BlockSpec((count, rows + EXTRA, half), lambda k: (k, 0, 0)),
        out_shape=jax.ShapeDtypeStruct((steps, rows + EXTRA, half), jnp.bfloat16),
        compiler_params=pltpu.CompilerParams(
            dimension_semantics=("arbitrary",), vmem_limit_bytes=32 * 1024 * 1024
        ),
        name="mix",
    )(own_w, other_w, own_d, other_d)


def shards(noise, data):
    n_row, n_col = lax.axis_size("row"), lax.axis_size("col")
    rows, half = noise.shape
    columns = data.shape[0]
    width = half * n_col
    core_word = jnp.full((1,), lax.rem(lax.axis_index("col"), CORES), jnp.int32)

    peer = lax.ppermute(noise, "col", SWAP)
    low = core_word[0] == 0
    pair = jnp.concatenate([jnp.where(low, noise, peer), jnp.where(low, peer, noise)], axis=1)
    latents = lax.all_to_all(
        jnp.broadcast_to(pair[None], (CHIPS,) + pair.shape), AXES, 0, 0, axis_index_groups=PLANE
    )
    forth = back = data
    chunks = [data]
    for far in range(1, Z // 2 + 1):
        forth = lax.ppermute(forth, "row", FORTH)
        chunks.append(forth)
        if far < Z // 2:
            back = lax.ppermute(back, "row", BACK)
            chunks.append(back)

    carry = None
    for call in range(Z // STEP):
        now = chunks[call * STEP : (call + 1) * STEP]
        carry = cost_step(core_word, latents, now, call, carry, 1.0 / (width * blur))
    scores, own_d, sent = carry
    other_d = lax.ppermute(sent, "col", SWAP)

    shift = math.log(rows * n_row / (columns * n_col))
    f = g = None
    for step in range(ITERS):
        if step == 0:
            top = jnp.max(scores, axis=1)
            total = jnp.sum(jnp.exp(scores - top[:, None]), axis=1)
            pairs = gathered(jnp.stack([top, total]), "col", n_col)
            top = jnp.max(pairs[:, 0], axis=0)
            f = -top - jnp.log(jnp.sum(pairs[:, 1] * jnp.exp(pairs[:, 0] - top), axis=0))
            shifted = scores + f[:, None]
            top = jnp.max(shifted, axis=0)
            total = jnp.sum(jnp.exp(shifted - top[None, :]), axis=0)
            pairs = gathered(jnp.stack([top, total]), "row", n_row)
            top = jnp.max(pairs[:, 0], axis=0)
            g = shift - top - jnp.log(jnp.sum(pairs[:, 1] * jnp.exp(pairs[:, 0] - top), axis=0))
        else:
            total = jnp.sum(jnp.exp(scores + f[:, None] + g[None, :]), axis=1)
            f = f - jnp.log(jnp.sum(gathered(total[None], "col", n_col), axis=(0, 1)))
            total = jnp.sum(jnp.exp(scores + f[:, None] + g[None, :]), axis=0)
            g = g + shift - jnp.log(jnp.sum(gathered(total[None], "row", n_row), axis=(0, 1)))

    own_w = jnp.exp(scores + f[:, None] + g[None, :]).astype(jnp.bfloat16)
    other_w = lax.ppermute(own_w, "col", SWAP)
    pieces = mixed(own_w, other_w, own_d, other_d)
    landed = lax.all_to_all(pieces, AXES, 0, 0, axis_index_groups=PLANE)
    summed = jnp.sum(landed.astype(jnp.float32), axis=0)
    mass = jnp.sum(summed[rows:].reshape(-1)[: 3 * rows].reshape(3, rows), axis=0)
    target = (summed[:rows] / mass[:, None] - noise.astype(jnp.float32)).astype(jnp.bfloat16)
    return (target, f * blur, g * blur)


def solution(mesh):
    return jax.shard_map(
        shards,
        mesh=mesh,
        in_specs=(P("row", "col"), P("col", "row")),
        out_specs=(P("row", "col"), P("row"), P("col")),
        check_vma=False,
    )
```

```python
import functools
import math

import jax
import jax.numpy as jnp
from jax import lax
from jax.experimental import pallas as pl
from jax.experimental.pallas import tpu as pltpu
from jax.sharding import PartitionSpec as P

ITERS = 4
blur = 0.01
X, Y, CORES, Z = 4, 4, 2, 16
CHIPS = X * Y
COLS = CHIPS * CORES
EXTRA = 16
TURN = 5
CALLS = [(0, 4), (4, 4), (8, 4), (12, 2), (14, 2)]
AXES = ("row", "col")

ORDER = [0]
for far in range(1, Z // 2):
    ORDER += [Z - far, far]
ORDER.append(Z // 2)

PLANE = [
    [z * COLS + (z + k) % CHIPS * CORES + core for k in ORDER] for z in range(Z) for core in range(CORES)
]
SWAP = [(index, index ^ 1) for index in range(COLS)]
FORTH = [(z, (z + 1) % Z) for z in range(Z)]
BACK = [(z, (z - 1) % Z) for z in range(Z)]
LAST = (((1,), (1,)), ((), ()))


def gathered(value, axis, count):
    copies = jnp.broadcast_to(value[None], (count,) + value.shape)
    return lax.all_to_all(copies, axis, 0, 0)


def squares(wide):
    wide = wide.astype(jnp.float32)
    wide = wide * wide
    high = wide.astype(jnp.bfloat16)
    return high, (wide - high.astype(jnp.float32)).astype(jnp.bfloat16)


def cost_kernel(core_ref, own_ref, other_ref, *refs, first, scale):
    size = own_ref.shape[0]
    data_refs, refs = refs[:size], refs[size:]
    if not first:
        acc_ref, refs = refs[0], refs[3:]
    out_ref, keep_ref, sent_ref = refs
    low = core_ref[0] == 0
    half = own_ref.shape[2]
    rows, columns = [], []
    for k in range(size):
        own, other = own_ref[k], other_ref[k]
        rows += [jnp.where(low, own, other), jnp.where(low, other, own)]
        chunk = data_refs[k][...]
        columns.append(chunk)
        left, right = chunk[:, :half], chunk[:, half:]
        keep_ref[k] = jnp.where(low, left, right)
        sent_ref[k] = jnp.where(low, right, left)
    rows = jnp.concatenate(rows, axis=1)
    columns = jnp.concatenate(columns, axis=1)
    inner = lax.dot_general(rows, columns, LAST, preferred_element_type=jnp.float32)
    width = rows.shape[1]
    ones = jnp.ones((8, width), jnp.bfloat16)
    wall = jnp.ones((width, 128), jnp.bfloat16)
    high, rest = squares(columns)
    ysq = lax.dot_general(ones, high, LAST, preferred_element_type=jnp.float32)
    ysq += lax.dot_general(ones, rest, LAST, preferred_element_type=jnp.float32)
    high, rest = squares(rows)
    xsq = jnp.dot(high, wall, preferred_element_type=jnp.float32)
    xsq += jnp.dot(rest, wall, preferred_element_type=jnp.float32)
    part = (2.0 * inner - xsq[:, :1] - ysq[:1, :]) * scale
    out_ref[...] = part if first else acc_ref[...] + part


def cost_step(core, own, other, chunks, start, carry, scale):
    size = len(chunks)
    block = start // size
    total, rows, half = own.shape
    columns, width = chunks[0].shape
    first = carry is None
    part = pl.BlockSpec((size, rows, half), lambda i, core: (block, 0, 0))
    part_d = pl.BlockSpec((size, columns, half), lambda i, core: (block, 0, 0))
    tile = pl.BlockSpec((rows, columns), lambda i, core: (0, 0))
    whole = pl.BlockSpec(memory_space=pltpu.HBM)
    in_specs = [part, part] + [pl.BlockSpec((columns, width), lambda i, core: (0, 0))] * size
    args = [core, own, other, *chunks]
    aliases = {}
    if not first:
        aliases = {len(args) + k: k for k in range(3)}
        in_specs += [tile, whole, whole]
        args += list(carry)
    halves = jax.ShapeDtypeStruct((total, columns, half), jnp.bfloat16)
    return pl.pallas_call(
        functools.partial(cost_kernel, first=first, scale=scale),
        grid_spec=pltpu.PrefetchScalarGridSpec(
            num_scalar_prefetch=1, grid=(1,), in_specs=in_specs, out_specs=[tile, part_d, part_d]
        ),
        out_shape=[jax.ShapeDtypeStruct((rows, columns), jnp.float32), halves, halves],
        input_output_aliases=aliases,
        compiler_params=pltpu.CompilerParams(
            dimension_semantics=("arbitrary",), vmem_limit_bytes=28 * 1024 * 1024
        ),
        cost_estimate=pl.CostEstimate(
            flops=2 * rows * columns * width * size, bytes_accessed=6 * 1024 * 1024, transcendentals=0
        ),
        name="cost",
    )(*args)


def mix_kernel(own_s_ref, other_s_ref, f_ref, g_ref, own_d_ref, other_d_ref, out_ref, plan, tail_ref):
    rows, columns = own_s_ref.shape
    count, _, half = own_d_ref.shape

    @pl.when(pl.program_id(0) == 0)
    def _():
        f = f_ref[...]
        own = jnp.exp(own_s_ref[...] + f + g_ref[:1, :]).astype(jnp.bfloat16)
        other = jnp.exp(other_s_ref[...] + f + g_ref[1:2, :]).astype(jnp.bfloat16)
        plan[:, :columns] = own
        plan[:, columns:] = other
        ones = jnp.ones((EXTRA, columns), jnp.bfloat16)
        left = lax.dot_general(ones, own, LAST, preferred_element_type=jnp.float32)
        left += lax.dot_general(ones, other, LAST, preferred_element_type=jnp.float32)
        line = lax.broadcasted_iota(jnp.int32, (EXTRA, half), 0)
        tail = jnp.zeros((EXTRA, half), jnp.float32)
        pieces = rows // half
        for part in range(3):
            rounded = left.astype(jnp.bfloat16).astype(jnp.float32)
            left = left - rounded
            for k in range(pieces):
                tail = jnp.where(
                    line == part * pieces + k, rounded[:, k * half : (k + 1) * half], tail
                )
        tail_ref[...] = tail.astype(jnp.bfloat16)

    own_d = jnp.concatenate([own_d_ref[k] for k in range(count)], axis=1)
    other_d = jnp.concatenate([other_d_ref[k] for k in range(count)], axis=1)
    both = jnp.concatenate([own_d, other_d], axis=0)
    total = jnp.dot(plan[...], both, preferred_element_type=jnp.float32)
    for k in range(count):
        out_ref[k, :rows, :] = total[:, k * half : (k + 1) * half].astype(jnp.bfloat16)
        out_ref[k, rows:, :] = tail_ref[...]


def mixed(own_s, other_s, f, g, own_d, other_d):
    steps, columns, half = other_d.shape
    rows = own_s.shape[0]
    count = 4
    tile = pl.BlockSpec((rows, columns), lambda k: (0, 0))
    part = pl.BlockSpec((count, columns, half), lambda k: (k, 0, 0))
    return pl.pallas_call(
        mix_kernel,
        grid=(steps // count,),
        in_specs=[
            tile,
            tile,
            pl.BlockSpec((rows, 1), lambda k: (0, 0)),
            pl.BlockSpec((2, columns), lambda k: (0, 0)),
            part,
            part,
        ],
        out_specs=pl.BlockSpec((count, rows + EXTRA, half), lambda k: (k, 0, 0)),
        out_shape=jax.ShapeDtypeStruct((steps, rows + EXTRA, half), jnp.bfloat16),
        scratch_shapes=[
            pltpu.VMEM((rows, 2 * columns), jnp.bfloat16),
            pltpu.VMEM((EXTRA, half), jnp.bfloat16),
        ],
        compiler_params=pltpu.CompilerParams(
            dimension_semantics=("arbitrary",), vmem_limit_bytes=28 * 1024 * 1024
        ),
        name="mix",
    )(own_s, other_s, f[:, None], g, own_d, other_d)


def shards(noise, data):
    n_row, n_col = lax.axis_size("row"), lax.axis_size("col")
    rows, half = noise.shape
    columns = data.shape[0]
    width = half * n_col
    core_word = jnp.full((1,), lax.rem(lax.axis_index("col"), CORES), jnp.int32)

    own = lax.all_to_all(
        jnp.broadcast_to(noise[None], (CHIPS,) + noise.shape), AXES, 0, 0, axis_index_groups=PLANE
    )
    forth = back = data
    chunks = [data]
    carry = other = None

    def cost(call):
        start, size = CALLS[call]
        now = chunks[start : start + size]
        return cost_step(core_word, own, other, now, start, carry, 1.0 / (width * blur))

    for far in range(1, Z // 2 + 1):
        forth = lax.ppermute(forth, "row", FORTH)
        if far == TURN:
            own, back = lax.optimization_barrier((own, back))
            other = lax.ppermute(own, "col", SWAP)
        if Z // 2 - 3 < far < Z // 2:
            carry = cost(far - Z // 2 + 2)
            total, back = lax.optimization_barrier((carry[0], back))
            carry = (total,) + tuple(carry[1:])
        if far < Z // 2:
            back = lax.ppermute(back, "row", BACK)
            forth, back = lax.optimization_barrier((forth, back))
            chunks += [forth, back]
    chunks.append(forth)
    for call in range(2, len(CALLS)):
        carry = cost(call)
    scores, own_d, sent = carry
    other_scores = lax.ppermute(scores, "col", SWAP)
    other_d = lax.ppermute(sent, "col", SWAP)

    shift = math.log(rows * n_row / (columns * n_col))
    f = g = None
    for step in range(ITERS):
        if step == 0:
            top = jnp.max(scores, axis=1)
            total = jnp.sum(jnp.exp(scores - top[:, None]), axis=1)
            pairs = gathered(jnp.stack([top, total]), "col", n_col)
            top = jnp.max(pairs[:, 0], axis=0)
            f = -top - jnp.log(jnp.sum(pairs[:, 1] * jnp.exp(pairs[:, 0] - top), axis=0))
            shifted = scores + f[:, None]
            top = jnp.max(shifted, axis=0)
            total = jnp.sum(jnp.exp(shifted - top[None, :]), axis=0)
            pairs = gathered(jnp.stack([top, total]), "row", n_row)
            top = jnp.max(pairs[:, 0], axis=0)
            g = shift - top - jnp.log(jnp.sum(pairs[:, 1] * jnp.exp(pairs[:, 0] - top), axis=0))
            continue
        last = step == ITERS - 1
        total = jnp.sum(jnp.exp(scores + f[:, None] + g[None, :]), axis=1)
        if last:
            other_g = lax.ppermute(g, "col", SWAP)
        f = f - jnp.log(jnp.sum(gathered(total[None], "col", n_col), axis=(0, 1)))
        total = jnp.sum(jnp.exp(scores + f[:, None] + g[None, :]), axis=0)[None]
        if last:
            extra = jnp.sum(jnp.exp(other_scores + f[:, None] + other_g[None, :]), axis=0)
            total = jnp.concatenate([total, extra[None]])
        total = jnp.sum(gathered(total, "row", n_row), axis=0)
        if last:
            both_g = jnp.stack([g, other_g]) + shift - jnp.log(total)
            g = both_g[0]
        else:
            g = g + shift - jnp.log(total[0])

    pieces = mixed(scores, other_scores, f, both_g, own_d, other_d)
    landed = lax.all_to_all(pieces, AXES, 0, 0, axis_index_groups=PLANE)
    summed = jnp.sum(landed.astype(jnp.float32), axis=0)
    mass = jnp.sum(summed[rows:].reshape(-1)[: 3 * rows].reshape(3, rows), axis=0)
    target = (summed[:rows] / mass[:, None] - noise.astype(jnp.float32)).astype(jnp.bfloat16)
    return (target, f * blur, g * blur)


def solution(mesh):
    return jax.shard_map(
        shards,
        mesh=mesh,
        in_specs=(P("row", "col"), P("col", "row")),
        out_specs=(P("row", "col"), P("row"), P("col")),
        check_vma=False,
    )
```

```python
import functools
import math

import jax
import jax.numpy as jnp
from jax import lax
from jax.experimental import pallas as pl
from jax.experimental.pallas import tpu as pltpu
from jax.sharding import PartitionSpec as P

ITERS = 4
blur = 0.01
X, Y, CORES, Z = 4, 4, 2, 16
CHIPS = X * Y
COLS = CHIPS * CORES
EXTRA = 16
CALLS = [(0, 4), (4, 4), (8, 4), (12, 2), (14, 2)]
GRANT = 56 * 1024 * 1024
AXES = ("row", "col")

ORDER = [0]
for far in range(1, Z // 2):
    ORDER += [Z - far, far]
ORDER.append(Z // 2)

PLANE = [
    [z * COLS + (z + k) % CHIPS * CORES + core for k in ORDER] for z in range(Z) for core in range(CORES)
]
SWAP = [(index, index ^ 1) for index in range(COLS)]
FORTH = [(z, (z + 1) % Z) for z in range(Z)]
BACK = [(z, (z - 1) % Z) for z in range(Z)]
LAST = (((1,), (1,)), ((), ()))


def gathered(value, axis, count):
    copies = jnp.broadcast_to(value[None], (count,) + value.shape)
    return lax.all_to_all(copies, axis, 0, 0)


def cost_kernel(core_ref, noise_ref, *refs, first, last, scale):
    size = noise_ref.shape[0]
    data_refs, refs = refs[:size], refs[size:]
    if not first:
        acc_ref, x_acc_ref, y_acc_ref, refs = refs[0], refs[3], refs[4], refs[5:]
    out_ref, keep_ref, sent_ref, x_ref, y_ref = refs
    low = core_ref[0] == 0
    half = noise_ref.shape[3]
    rows, columns = [], []
    xsq = jnp.zeros(x_ref.shape, jnp.float32) if first else x_acc_ref[...]
    ysq = jnp.zeros(y_ref.shape, jnp.float32) if first else y_acc_ref[...]
    for k in range(size):
        own, other = noise_ref[k, 0], noise_ref[k, 1]
        rows += [jnp.where(low, own, other), jnp.where(low, other, own)]
        chunk = data_refs[k][...]
        columns.append(chunk)
        left, right = chunk[:, :half], chunk[:, half:]
        keep_ref[k] = jnp.where(low, left, right)
        sent_ref[k] = jnp.where(low, right, left)
        xsq += own.astype(jnp.float32) ** 2 + other.astype(jnp.float32) ** 2
        ysq += left.astype(jnp.float32) ** 2 + right.astype(jnp.float32) ** 2
    rows = jnp.concatenate(rows, axis=1)
    columns = jnp.concatenate(columns, axis=1)
    total = lax.dot_general(rows, columns, LAST, preferred_element_type=jnp.float32)
    if not first:
        total += acc_ref[...]
    if last:
        xsq_column = jnp.sum(xsq, axis=1, keepdims=True)
        ysq_row = jnp.sum(ysq.T, axis=0, keepdims=True)
        total = (2.0 * total - xsq_column - ysq_row) * scale
    out_ref[...] = total
    x_ref[...] = xsq
    y_ref[...] = ysq


def cost_step(core, pairs, chunks, start, carry, scale):
    size = len(chunks)
    last = start + size == Z
    block = start // size
    total, _, rows, half = pairs.shape
    columns, width = chunks[0].shape
    first = carry is None
    part = pl.BlockSpec((size, CORES, rows, half), lambda i, core: (block, 0, 0, 0))
    part_d = pl.BlockSpec((size, columns, half), lambda i, core: (block, 0, 0))
    tile = pl.BlockSpec((rows, columns), lambda i, core: (0, 0))
    narrow = pl.BlockSpec((rows, half), lambda i, core: (0, 0))
    whole = pl.BlockSpec(memory_space=pl.ANY)
    in_specs = [part] + [pl.BlockSpec((columns, width), lambda i, core: (0, 0))] * size
    args = [core, pairs, *chunks]
    aliases = {}
    if not first:
        aliases = {len(args) + k: k for k in range(5)}
        in_specs += [tile, whole, whole, narrow, narrow]
        args += list(carry)
    halves = jax.ShapeDtypeStruct((total, columns, half), jnp.bfloat16)
    sums = jax.ShapeDtypeStruct((rows, half), jnp.float32)
    return pl.pallas_call(
        functools.partial(cost_kernel, first=first, last=last, scale=scale),
        grid_spec=pltpu.PrefetchScalarGridSpec(
            num_scalar_prefetch=1, grid=(1,), in_specs=in_specs, out_specs=[tile, part_d, part_d, narrow, narrow]
        ),
        out_shape=[jax.ShapeDtypeStruct((rows, columns), jnp.float32), halves, halves, sums, sums],
        input_output_aliases=aliases,
        compiler_params=pltpu.CompilerParams(
            dimension_semantics=("arbitrary",), vmem_limit_bytes=GRANT
        ),
        cost_estimate=pl.CostEstimate(
            flops=2 * rows * columns * width * size, bytes_accessed=6 * 1024 * 1024, transcendentals=0
        ),
        name="cost",
    )(*args)


def mix_kernel(own_s_ref, other_s_ref, f_ref, g_ref, own_d_ref, other_d_ref, out_ref, plan, tail_ref):
    rows, columns = own_s_ref.shape
    count, _, half = own_d_ref.shape

    @pl.when(pl.program_id(0) == 0)
    def _():
        f = f_ref[...]
        own = jnp.exp(own_s_ref[...] + f + g_ref[:1, :]).astype(jnp.bfloat16)
        other = jnp.exp(other_s_ref[...] + f + g_ref[1:2, :]).astype(jnp.bfloat16)
        plan[:, :columns] = own
        plan[:, columns:] = other
        ones = jnp.ones((EXTRA, columns), jnp.bfloat16)
        left = lax.dot_general(ones, own, LAST, preferred_element_type=jnp.float32)
        left += lax.dot_general(ones, other, LAST, preferred_element_type=jnp.float32)
        line = lax.broadcasted_iota(jnp.int32, (EXTRA, half), 0)
        tail = jnp.zeros((EXTRA, half), jnp.float32)
        pieces = rows // half
        for part in range(3):
            rounded = left.astype(jnp.bfloat16).astype(jnp.float32)
            left = left - rounded
            for k in range(pieces):
                tail = jnp.where(
                    line == part * pieces + k, rounded[:, k * half : (k + 1) * half], tail
                )
        tail_ref[...] = tail.astype(jnp.bfloat16)

    own_d = jnp.concatenate([own_d_ref[k] for k in range(count)], axis=1)
    other_d = jnp.concatenate([other_d_ref[k] for k in range(count)], axis=1)
    both = jnp.concatenate([own_d, other_d], axis=0)
    total = jnp.dot(plan[...], both, preferred_element_type=jnp.float32)
    for k in range(count):
        out_ref[k, :rows, :] = total[:, k * half : (k + 1) * half].astype(jnp.bfloat16)
        out_ref[k, rows:, :] = tail_ref[...]


def mixed(own_s, other_s, f, g, own_d, other_d):
    steps, columns, half = other_d.shape
    rows = own_s.shape[0]
    count = 4
    tile = pl.BlockSpec((rows, columns), lambda k: (0, 0))
    part = pl.BlockSpec((count, columns, half), lambda k: (k, 0, 0))
    return pl.pallas_call(
        mix_kernel,
        grid=(steps // count,),
        in_specs=[
            tile,
            tile,
            pl.BlockSpec((rows, 1), lambda k: (0, 0)),
            pl.BlockSpec((2, columns), lambda k: (0, 0)),
            part,
            part,
        ],
        out_specs=pl.BlockSpec((count, rows + EXTRA, half), lambda k: (k, 0, 0)),
        out_shape=jax.ShapeDtypeStruct((steps, rows + EXTRA, half), jnp.bfloat16),
        scratch_shapes=[
            pltpu.VMEM((rows, 2 * columns), jnp.bfloat16),
            pltpu.VMEM((EXTRA, half), jnp.bfloat16),
        ],
        compiler_params=pltpu.CompilerParams(
            dimension_semantics=("arbitrary",), vmem_limit_bytes=GRANT
        ),
        name="mix",
    )(own_s, other_s, f[:, None], g, own_d, other_d)


def shards(noise, data):
    n_row, n_col = lax.axis_size("row"), lax.axis_size("col")
    rows, half = noise.shape
    columns = data.shape[0]
    width = half * n_col
    core_word = jnp.full((1,), lax.rem(lax.axis_index("col"), CORES), jnp.int32)

    pair = jnp.stack([noise, lax.ppermute(noise, "col", SWAP)])
    pairs = lax.all_to_all(
        jnp.broadcast_to(pair[None], (CHIPS,) + pair.shape), AXES, 0, 0, axis_index_groups=PLANE
    )
    forth = back = data
    chunks = [data]
    carry = None

    def cost(call):
        start, size = CALLS[call]
        now = chunks[start : start + size]
        return cost_step(core_word, pairs, now, start, carry, 1.0 / (width * blur))

    for far in range(1, Z // 2 + 1):
        forth = lax.ppermute(forth, "row", FORTH)
        chunks.append(forth)
        if far < Z // 2:
            back = lax.ppermute(back, "row", BACK)
            chunks.append(back)
    for call in range(len(CALLS)):
        carry = cost(call)
    scores, own_d, sent = carry[:3]
    other_scores = lax.ppermute(scores, "col", SWAP)
    other_d = lax.ppermute(sent, "col", SWAP)

    shift = math.log(rows * n_row / (columns * n_col))
    f = g = None
    for step in range(ITERS):
        if step == 0:
            top = jnp.max(scores, axis=1)
            total = jnp.sum(jnp.exp(scores - top[:, None]), axis=1)
            pairs = gathered(jnp.stack([top, total]), "col", n_col)
            top = jnp.max(pairs[:, 0], axis=0)
            f = -top - jnp.log(jnp.sum(pairs[:, 1] * jnp.exp(pairs[:, 0] - top), axis=0))
            shifted = scores + f[:, None]
            top = jnp.max(shifted, axis=0)
            total = jnp.sum(jnp.exp(shifted - top[None, :]), axis=0)
            pairs = gathered(jnp.stack([top, total]), "row", n_row)
            top = jnp.max(pairs[:, 0], axis=0)
            g = shift - top - jnp.log(jnp.sum(pairs[:, 1] * jnp.exp(pairs[:, 0] - top), axis=0))
            continue
        last = step == ITERS - 1
        total = jnp.sum(jnp.exp(scores + f[:, None] + g[None, :]), axis=1)
        if last:
            other_g = lax.ppermute(g, "col", SWAP)
        f = f - jnp.log(jnp.sum(gathered(total[None], "col", n_col), axis=(0, 1)))
        total = jnp.sum(jnp.exp(scores + f[:, None] + g[None, :]), axis=0)[None]
        if last:
            extra = jnp.sum(jnp.exp(other_scores + f[:, None] + other_g[None, :]), axis=0)
            total = jnp.concatenate([total, extra[None]])
        total = jnp.sum(gathered(total, "row", n_row), axis=0)
        if last:
            both_g = jnp.stack([g, other_g]) + shift - jnp.log(total)
            g = both_g[0]
        else:
            g = g + shift - jnp.log(total[0])

    pieces = mixed(scores, other_scores, f, both_g, own_d, other_d)
    landed = lax.all_to_all(pieces, AXES, 0, 0, axis_index_groups=PLANE)
    summed = jnp.sum(landed.astype(jnp.float32), axis=0)
    mass = jnp.sum(summed[rows:].reshape(-1)[: 3 * rows].reshape(3, rows), axis=0)
    target = (summed[:rows] / mass[:, None] - noise.astype(jnp.float32)).astype(jnp.bfloat16)
    return (target, f * blur, g * blur)


def solution(mesh):
    return jax.shard_map(
        shards,
        mesh=mesh,
        in_specs=(P("row", "col"), P("col", "row")),
        out_specs=(P("row", "col"), P("row"), P("col")),
        check_vma=False,
    )
```

```python
import functools
import math

import jax
import jax.numpy as jnp
from jax import lax
from jax.experimental import pallas as pl
from jax.experimental.pallas import tpu as pltpu
from jax.sharding import PartitionSpec as P

ITERS = 4
blur = 0.01
X, Y, CORES, Z = 4, 4, 2, 16
CHIPS = X * Y
COLS = CHIPS * CORES
EXTRA = 16
TURN = 6
CALLS = [(0, 14), (14, 2)]
GRANT = 56 * 1024 * 1024
AXES = ("row", "col")

ORDER = [0]
for far in range(1, Z // 2):
    ORDER += [Z - far, far]
ORDER.append(Z // 2)

PLANE = [
    [z * COLS + (z + k) % CHIPS * CORES + core for k in ORDER] for z in range(Z) for core in range(CORES)
]
SWAP = [(index, index ^ 1) for index in range(COLS)]
FORTH = [(z, (z + 1) % Z) for z in range(Z)]
BACK = [(z, (z - 1) % Z) for z in range(Z)]
LAST = (((1,), (1,)), ((), ()))


def gathered(value, axis, count):
    copies = jnp.broadcast_to(value[None], (count,) + value.shape)
    return lax.all_to_all(copies, axis, 0, 0)


def cost_kernel(core_ref, own_ref, other_ref, *refs, first, last, scale):
    size = own_ref.shape[0]
    data_refs, refs = refs[:size], refs[size:]
    if not first:
        acc_ref, x_acc_ref, y_acc_ref, refs = refs[0], refs[3], refs[4], refs[5:]
    out_ref, keep_ref, sent_ref = refs[:3]
    low = core_ref[0] == 0
    half = own_ref.shape[2]
    rows, columns = [], []
    xsq = ysq = 0.0
    if not first:
        xsq, ysq = x_acc_ref[...], y_acc_ref[...]
    for k in range(size):
        own, other = own_ref[k], other_ref[k]
        rows += [jnp.where(low, own, other), jnp.where(low, other, own)]
        chunk = data_refs[k][...]
        columns.append(chunk)
        left, right = chunk[:, :half], chunk[:, half:]
        keep_ref[k] = jnp.where(low, left, right)
        sent_ref[k] = jnp.where(low, right, left)
        xsq += own.astype(jnp.float32) ** 2 + other.astype(jnp.float32) ** 2
        ysq += left.astype(jnp.float32) ** 2 + right.astype(jnp.float32) ** 2
    rows = jnp.concatenate(rows, axis=1)
    columns = jnp.concatenate(columns, axis=1)
    total = lax.dot_general(rows, columns, LAST, preferred_element_type=jnp.float32)
    if not first:
        total += acc_ref[...]
    if last:
        xsq_column = jnp.sum(xsq, axis=1, keepdims=True)
        ysq_row = jnp.sum(ysq.T, axis=0, keepdims=True)
        total = (2.0 * total - xsq_column - ysq_row) * scale
        lanes = range(0, total.shape[1], half)
        top = functools.reduce(jnp.maximum, [total[:, k : k + half] for k in lanes])
        grown = jnp.exp(total - jnp.max(top, axis=1, keepdims=True))
        grown = functools.reduce(jnp.add, [grown[:, k : k + half] for k in lanes])
        refs[3][0:1, :] = jnp.max(top.T, axis=0, keepdims=True)
        refs[3][1:2, :] = jnp.sum(grown.T, axis=0, keepdims=True)
    else:
        refs[3][...] = xsq
        refs[4][...] = ysq
    out_ref[...] = total


def cost_step(core, own, other, chunks, start, carry, scale):
    size = len(chunks)
    last = start + size == Z
    block = start // size
    total, rows, half = own.shape
    columns, width = chunks[0].shape
    first = carry is None
    part = pl.BlockSpec((size, rows, half), lambda i, core: (block, 0, 0))
    part_d = pl.BlockSpec((size, columns, half), lambda i, core: (block, 0, 0))
    tile = pl.BlockSpec((rows, columns), lambda i, core: (0, 0))
    narrow = pl.BlockSpec((rows, half), lambda i, core: (0, 0))
    whole = pl.BlockSpec(memory_space=pl.ANY)
    in_specs = [part, part] + [pl.BlockSpec((columns, width), lambda i, core: (0, 0))] * size
    args = [core, own, other, *chunks]
    aliases = {}
    if not first:
        aliases = {len(args) + k: k for k in ((1, 2) if last else range(5))}
        in_specs += [tile, whole, whole, narrow, narrow]
        args += list(carry)
    halves = jax.ShapeDtypeStruct((total, columns, half), jnp.bfloat16)
    stats = pl.BlockSpec((2, rows), lambda i, core: (0, 0))
    sums = [jax.ShapeDtypeStruct((rows, half), jnp.float32)] * 2
    if last:
        sums = [jax.ShapeDtypeStruct((2, rows), jnp.float32)]
    return pl.pallas_call(
        functools.partial(cost_kernel, first=first, last=last, scale=scale),
        grid_spec=pltpu.PrefetchScalarGridSpec(
            num_scalar_prefetch=1, grid=(1,), in_specs=in_specs, out_specs=[tile, part_d, part_d] + ([stats] if last else [narrow] * 2)
        ),
        out_shape=[jax.ShapeDtypeStruct((rows, columns), jnp.float32), halves, halves, *sums],
        input_output_aliases=aliases,
        compiler_params=pltpu.CompilerParams(
            dimension_semantics=("arbitrary",), vmem_limit_bytes=GRANT
        ),
        cost_estimate=pl.CostEstimate(
            flops=2 * rows * columns * width * size, bytes_accessed=6 * 1024 * 1024, transcendentals=0
        ),
        name="cost",
    )(*args)


def mix_kernel(own_s_ref, other_s_ref, f_ref, g_ref, own_d_ref, other_d_ref, out_ref, plan, tail_ref):
    rows, columns = own_s_ref.shape
    count, _, half = own_d_ref.shape

    @pl.when(pl.program_id(0) == 0)
    def _():
        f = f_ref[...]
        own = jnp.exp(own_s_ref[...] + f + g_ref[:1, :]).astype(jnp.bfloat16)
        other = jnp.exp(other_s_ref[...] + f + g_ref[1:2, :]).astype(jnp.bfloat16)
        plan[:, :columns] = own
        plan[:, columns:] = other
        ones = jnp.ones((EXTRA, columns), jnp.bfloat16)
        left = lax.dot_general(ones, own, LAST, preferred_element_type=jnp.float32)
        left += lax.dot_general(ones, other, LAST, preferred_element_type=jnp.float32)
        line = lax.broadcasted_iota(jnp.int32, (EXTRA, half), 0)
        tail = jnp.zeros((EXTRA, half), jnp.float32)
        pieces = rows // half
        for part in range(3):
            rounded = left.astype(jnp.bfloat16).astype(jnp.float32)
            left = left - rounded
            for k in range(pieces):
                tail = jnp.where(
                    line == part * pieces + k, rounded[:, k * half : (k + 1) * half], tail
                )
        tail_ref[...] = tail.astype(jnp.bfloat16)

    own_d = jnp.concatenate([own_d_ref[k] for k in range(count)], axis=1)
    other_d = jnp.concatenate([other_d_ref[k] for k in range(count)], axis=1)
    both = jnp.concatenate([own_d, other_d], axis=0)
    total = jnp.dot(plan[...], both, preferred_element_type=jnp.float32)
    for k in range(count):
        out_ref[k, :rows, :] = total[:, k * half : (k + 1) * half].astype(jnp.bfloat16)
        out_ref[k, rows:, :] = tail_ref[...]


def mixed(own_s, other_s, f, g, own_d, other_d):
    steps, columns, half = other_d.shape
    rows = own_s.shape[0]
    count = 4
    tile = pl.BlockSpec((rows, columns), lambda k: (0, 0))
    part = pl.BlockSpec((count, columns, half), lambda k: (k, 0, 0))
    return pl.pallas_call(
        mix_kernel,
        grid=(steps // count,),
        in_specs=[
            tile,
            tile,
            pl.BlockSpec((rows, 1), lambda k: (0, 0)),
            pl.BlockSpec((2, columns), lambda k: (0, 0)),
            part,
            part,
        ],
        out_specs=pl.BlockSpec((count, rows + EXTRA, half), lambda k: (k, 0, 0)),
        out_shape=jax.ShapeDtypeStruct((steps, rows + EXTRA, half), jnp.bfloat16),
        scratch_shapes=[
            pltpu.VMEM((rows, 2 * columns), jnp.bfloat16),
            pltpu.VMEM((EXTRA, half), jnp.bfloat16),
        ],
        compiler_params=pltpu.CompilerParams(
            dimension_semantics=("arbitrary",), vmem_limit_bytes=GRANT
        ),
        name="mix",
    )(own_s, other_s, f[:, None], g, own_d, other_d)


def shards(noise, data):
    n_row, n_col = lax.axis_size("row"), lax.axis_size("col")
    rows, half = noise.shape
    columns = data.shape[0]
    width = half * n_col
    core_word = jnp.full((1,), lax.rem(lax.axis_index("col"), CORES), jnp.int32)

    own = lax.all_to_all(
        jnp.broadcast_to(noise[None], (CHIPS,) + noise.shape), AXES, 0, 0, axis_index_groups=PLANE
    )
    forth = back = data
    chunks = [data]
    for far in range(1, Z // 2 + 1):
        forth = lax.ppermute(forth, "row", FORTH)
        chunks.append(forth)
        if far < Z // 2:
            back = lax.ppermute(back, "row", BACK)
            chunks.append(back)
        if far == TURN:
            own, _, _ = lax.optimization_barrier((own, forth, back))
            other = lax.ppermute(own, "col", SWAP)
    carry = None

    def cost(call):
        start, size = CALLS[call]
        now = chunks[start : start + size]
        return cost_step(core_word, own, other, now, start, carry, 1.0 / (width * blur))

    for call in range(len(CALLS)):
        carry = cost(call)
    scores, own_d, sent, stats = carry
    other_scores = lax.ppermute(scores, "col", SWAP)
    other_d = lax.ppermute(sent, "col", SWAP)

    shift = math.log(rows * n_row / (columns * n_col))
    f = g = None
    for step in range(ITERS):
        if step == 0:
            pairs = gathered(stats, "col", n_col)
            top = jnp.max(pairs[:, 0], axis=0)
            f = -top - jnp.log(jnp.sum(pairs[:, 1] * jnp.exp(pairs[:, 0] - top), axis=0))
            shifted = scores + f[:, None]
            top = jnp.max(shifted, axis=0)
            total = jnp.sum(jnp.exp(shifted - top[None, :]), axis=0)
            pairs = gathered(jnp.stack([top, total]), "row", n_row)
            top = jnp.max(pairs[:, 0], axis=0)
            g = shift - top - jnp.log(jnp.sum(pairs[:, 1] * jnp.exp(pairs[:, 0] - top), axis=0))
            continue
        last = step == ITERS - 1
        total = jnp.sum(jnp.exp(scores + f[:, None] + g[None, :]), axis=1)
        if last:
            other_g = lax.ppermute(g, "col", SWAP)
        f = f - jnp.log(jnp.sum(gathered(total[None], "col", n_col), axis=(0, 1)))
        total = jnp.sum(jnp.exp(scores + f[:, None] + g[None, :]), axis=0)[None]
        if last:
            extra = jnp.sum(jnp.exp(other_scores + f[:, None] + other_g[None, :]), axis=0)
            total = jnp.concatenate([total, extra[None]])
        total = jnp.sum(gathered(total, "row", n_row), axis=0)
        if last:
            both_g = jnp.stack([g, other_g]) + shift - jnp.log(total)
            g = both_g[0]
        else:
            g = g + shift - jnp.log(total[0])

    pieces = mixed(scores, other_scores, f, both_g, own_d, other_d)
    landed = lax.all_to_all(pieces, AXES, 0, 0, axis_index_groups=PLANE)
    summed = jnp.sum(landed.astype(jnp.float32), axis=0)
    mass = jnp.sum(summed[rows:].reshape(-1)[: 3 * rows].reshape(3, rows), axis=0)
    target = (summed[:rows] / mass[:, None] - noise.astype(jnp.float32)).astype(jnp.bfloat16)
    return (target, f * blur, g * blur)


def solution(mesh):
    return jax.shard_map(
        shards,
        mesh=mesh,
        in_specs=(P("row", "col"), P("col", "row")),
        out_specs=(P("row", "col"), P("row"), P("col")),
        check_vma=False,
    )
```

```python
import functools
import math

import jax
import jax.numpy as jnp
from jax import lax
from jax.experimental import pallas as pl
from jax.experimental.pallas import tpu as pltpu
from jax.sharding import PartitionSpec as P

ITERS = 4
blur = 0.01
X, Y, CORES, Z = 4, 4, 2, 16
CHIPS = X * Y
COLS = CHIPS * CORES
EXTRA = 16
CALLS = [(0, 14), (14, 2)]
GRANT = 56 * 1024 * 1024
AXES = ("row", "col")

ORDER = [0]
for far in range(1, Z // 2):
    ORDER += [Z - far, far]
ORDER.append(Z // 2)

PLANE = [
    [z * COLS + (z + k) % CHIPS * CORES + core for k in ORDER] for z in range(Z) for core in range(CORES)
]
WHOLE = [
    [z * COLS + (z + k) % CHIPS * CORES + core for k in ORDER for core in range(CORES)] for z in range(Z)
]
SWAP = [(index, index ^ 1) for index in range(COLS)]
FORTH = [(z, (z + 1) % Z) for z in range(Z)]
BACK = [(z, (z - 1) % Z) for z in range(Z)]
LAST = (((1,), (1,)), ((), ()))


def gathered(value, axis, count):
    copies = jnp.broadcast_to(value[None], (count,) + value.shape)
    return lax.all_to_all(copies, axis, 0, 0)


def cost_kernel(core_ref, noise_ref, *refs, first, last, scale):
    size = noise_ref.shape[0]
    data_refs, refs = refs[:size], refs[size:]
    if not first:
        acc_ref, x_acc_ref, y_acc_ref, refs = refs[0], refs[3], refs[4], refs[5:]
    out_ref, keep_ref, sent_ref = refs[:3]
    low = core_ref[0] == 0
    half = noise_ref.shape[3]
    rows, columns = [], []
    xsq = ysq = 0.0
    if not first:
        xsq, ysq = x_acc_ref[...], y_acc_ref[...]
    for k in range(size):
        rows += [noise_ref[k, 0], noise_ref[k, 1]]
        chunk = data_refs[k][...]
        columns.append(chunk)
        left, right = chunk[:, :half], chunk[:, half:]
        keep_ref[k] = jnp.where(low, left, right)
        sent_ref[k] = jnp.where(low, right, left)
        xsq += rows[-2].astype(jnp.float32) ** 2 + rows[-1].astype(jnp.float32) ** 2
        ysq += left.astype(jnp.float32) ** 2 + right.astype(jnp.float32) ** 2
    rows = jnp.concatenate(rows, axis=1)
    columns = jnp.concatenate(columns, axis=1)
    total = lax.dot_general(rows, columns, LAST, preferred_element_type=jnp.float32)
    if not first:
        total += acc_ref[...]
    if last:
        xsq_column = jnp.sum(xsq, axis=1, keepdims=True)
        ysq_row = jnp.sum(ysq.T, axis=0, keepdims=True)
        total = (2.0 * total - xsq_column - ysq_row) * scale
        lanes = range(0, total.shape[1], half)
        top = functools.reduce(jnp.maximum, [total[:, k : k + half] for k in lanes])
        grown = jnp.exp(total - jnp.max(top, axis=1, keepdims=True))
        grown = functools.reduce(jnp.add, [grown[:, k : k + half] for k in lanes])
        refs[3][0:1, :] = jnp.max(top.T, axis=0, keepdims=True)
        refs[3][1:2, :] = jnp.sum(grown.T, axis=0, keepdims=True)
    else:
        refs[3][...] = xsq
        refs[4][...] = ysq
    out_ref[...] = total


def cost_step(core, pairs, chunks, start, carry, scale):
    size = len(chunks)
    last = start + size == Z
    block = start // size
    total, _, rows, half = pairs.shape
    columns, width = chunks[0].shape
    first = carry is None
    part = pl.BlockSpec((size, CORES, rows, half), lambda i, core: (block, 0, 0, 0))
    part_d = pl.BlockSpec((size, columns, half), lambda i, core: (block, 0, 0))
    tile = pl.BlockSpec((rows, columns), lambda i, core: (0, 0))
    narrow = pl.BlockSpec((rows, half), lambda i, core: (0, 0))
    whole = pl.BlockSpec(memory_space=pl.ANY)
    in_specs = [part] + [pl.BlockSpec((columns, width), lambda i, core: (0, 0))] * size
    args = [core, pairs, *chunks]
    aliases = {}
    if not first:
        aliases = {len(args) + k: k for k in ((1, 2) if last else range(5))}
        in_specs += [tile, whole, whole, narrow, narrow]
        args += list(carry)
    halves = jax.ShapeDtypeStruct((total, columns, half), jnp.bfloat16)
    stats = pl.BlockSpec((2, rows), lambda i, core: (0, 0))
    sums = [jax.ShapeDtypeStruct((rows, half), jnp.float32)] * 2
    if last:
        sums = [jax.ShapeDtypeStruct((2, rows), jnp.float32)]
    return pl.pallas_call(
        functools.partial(cost_kernel, first=first, last=last, scale=scale),
        grid_spec=pltpu.PrefetchScalarGridSpec(
            num_scalar_prefetch=1, grid=(1,), in_specs=in_specs, out_specs=[tile, part_d, part_d] + ([stats] if last else [narrow] * 2)
        ),
        out_shape=[jax.ShapeDtypeStruct((rows, columns), jnp.float32), halves, halves, *sums],
        input_output_aliases=aliases,
        compiler_params=pltpu.CompilerParams(
            dimension_semantics=("arbitrary",), vmem_limit_bytes=GRANT
        ),
        cost_estimate=pl.CostEstimate(
            flops=2 * rows * columns * width * size, bytes_accessed=6 * 1024 * 1024, transcendentals=0
        ),
        name="cost",
    )(*args)


def mix_kernel(own_s_ref, other_s_ref, f_ref, g_ref, own_d_ref, other_d_ref, out_ref, plan, tail_ref):
    rows, columns = own_s_ref.shape
    count, _, half = own_d_ref.shape

    @pl.when(pl.program_id(0) == 0)
    def _():
        f = jnp.broadcast_to(f_ref[...], (8, rows)).T[:, :1]
        own = jnp.exp(own_s_ref[...] + f + g_ref[:1, :]).astype(jnp.bfloat16)
        other = jnp.exp(other_s_ref[...] + f + g_ref[1:2, :]).astype(jnp.bfloat16)
        plan[:, :columns] = own
        plan[:, columns:] = other
        ones = jnp.ones((EXTRA, columns), jnp.bfloat16)
        left = lax.dot_general(ones, own, LAST, preferred_element_type=jnp.float32)
        left += lax.dot_general(ones, other, LAST, preferred_element_type=jnp.float32)
        line = lax.broadcasted_iota(jnp.int32, (EXTRA, half), 0)
        tail = jnp.zeros((EXTRA, half), jnp.float32)
        pieces = rows // half
        for part in range(3):
            rounded = left.astype(jnp.bfloat16).astype(jnp.float32)
            left = left - rounded
            for k in range(pieces):
                tail = jnp.where(
                    line == part * pieces + k, rounded[:, k * half : (k + 1) * half], tail
                )
        tail_ref[...] = tail.astype(jnp.bfloat16)

    own_d = jnp.concatenate([own_d_ref[k] for k in range(count)], axis=1)
    other_d = jnp.concatenate([other_d_ref[k] for k in range(count)], axis=1)
    both = jnp.concatenate([own_d, other_d], axis=0)
    total = jnp.dot(plan[...], both, preferred_element_type=jnp.float32)
    for k in range(count):
        out_ref[k, :rows, :] = total[:, k * half : (k + 1) * half].astype(jnp.bfloat16)
        out_ref[k, rows:, :] = tail_ref[...]


def mixed(own_s, other_s, f, g, own_d, other_d):
    steps, columns, half = other_d.shape
    rows = own_s.shape[0]
    count = 4
    tile = pl.BlockSpec((rows, columns), lambda k: (0, 0))
    part = pl.BlockSpec((count, columns, half), lambda k: (k, 0, 0))
    return pl.pallas_call(
        mix_kernel,
        grid=(steps // count,),
        in_specs=[
            tile,
            tile,
            pl.BlockSpec((1, rows), lambda k: (0, 0)),
            pl.BlockSpec((2, columns), lambda k: (0, 0)),
            part,
            part,
        ],
        out_specs=pl.BlockSpec((count, rows + EXTRA, half), lambda k: (k, 0, 0)),
        out_shape=jax.ShapeDtypeStruct((steps, rows + EXTRA, half), jnp.bfloat16),
        scratch_shapes=[
            pltpu.VMEM((rows, 2 * columns), jnp.bfloat16),
            pltpu.VMEM((EXTRA, half), jnp.bfloat16),
        ],
        compiler_params=pltpu.CompilerParams(
            dimension_semantics=("arbitrary",), vmem_limit_bytes=GRANT
        ),
        name="mix",
    )(own_s, other_s, f[None, :], g, own_d, other_d)


def shards(noise, data):
    n_row, n_col = lax.axis_size("row"), lax.axis_size("col")
    rows, half = noise.shape
    columns = data.shape[0]
    width = half * n_col
    core_word = jnp.full((1,), lax.rem(lax.axis_index("col"), CORES), jnp.int32)

    pairs = lax.all_to_all(
        jnp.broadcast_to(noise[None], (COLS,) + noise.shape), AXES, 0, 0, axis_index_groups=WHOLE
    ).reshape((CHIPS, CORES) + noise.shape)
    forth = back = data
    chunks = [data]
    for far in range(1, Z // 2 + 1):
        forth = lax.ppermute(forth, "row", FORTH)
        chunks.append(forth)
        if far < Z // 2:
            back = lax.ppermute(back, "row", BACK)
            chunks.append(back)
    carry = None

    def cost(call):
        start, size = CALLS[call]
        now = chunks[start : start + size]
        return cost_step(core_word, pairs, now, start, carry, 1.0 / (width * blur))

    for call in range(len(CALLS)):
        carry = cost(call)
    scores, own_d, sent, stats = carry
    other_scores = lax.ppermute(scores, "col", SWAP)
    other_d = lax.ppermute(sent, "col", SWAP)

    shift = math.log(rows * n_row / (columns * n_col))
    tiles = (scores, other_scores)
    f = g = None
    for step in range(ITERS):
        if step == 0:
            pairs = gathered(stats, "col", n_col)
            top = jnp.max(pairs[:, 0], axis=0)
            f = -top - jnp.log(jnp.sum(pairs[:, 1] * jnp.exp(pairs[:, 0] - top), axis=0))
            tops, totals = [], []
            for tile in tiles:
                shifted = tile + f[:, None]
                tops.append(jnp.max(shifted, axis=0))
                totals.append(jnp.sum(jnp.exp(shifted - tops[-1][None, :]), axis=0))
            pairs = gathered(jnp.stack(tops + totals), "row", n_row)
            top = jnp.max(pairs[:, :CORES], axis=0)
            g = shift - top - jnp.log(jnp.sum(pairs[:, CORES:] * jnp.exp(pairs[:, :CORES] - top), axis=0))
            g, other_d = lax.optimization_barrier((g, other_d))
        else:
            total = jnp.sum(jnp.exp(scores + f[:, None] + g[0][None, :]), axis=1)
            f = f - jnp.log(jnp.sum(gathered(total[None], "col", n_col), axis=(0, 1)))
            totals = [
                jnp.sum(jnp.exp(tile + f[:, None] + g[k][None, :]), axis=0) for k, tile in enumerate(tiles)
            ]
            g = g + shift - jnp.log(jnp.sum(gathered(jnp.stack(totals), "row", n_row), axis=0))

    pieces = mixed(scores, other_scores, f, g, own_d, other_d)
    landed = lax.all_to_all(pieces, AXES, 0, 0, axis_index_groups=PLANE)
    summed = jnp.sum(landed.astype(jnp.float32), axis=0)
    mass = jnp.sum(summed[rows:].reshape(-1)[: 3 * rows].reshape(3, rows), axis=0)
    target = (summed[:rows] / mass[:, None] - noise.astype(jnp.float32)).astype(jnp.bfloat16)
    return (target, f * blur, g[0] * blur)


def solution(mesh):
    return jax.shard_map(
        shards,
        mesh=mesh,
        in_specs=(P("row", "col"), P("col", "row")),
        out_specs=(P("row", "col"), P("row"), P("col")),
        check_vma=False,
    )
```

```python
import functools
import math

import jax
import jax.numpy as jnp
from jax import lax
from jax.experimental import pallas as pl
from jax.experimental.pallas import tpu as pltpu
from jax.sharding import PartitionSpec as P

ITERS = 4
blur = 0.01
X, Y, CORES, Z = 4, 4, 2, 16
CHIPS = X * Y
COLS = CHIPS * CORES
EXTRA = 16
CALLS = [(0, 14), (14, 2)]
GRANT = 56 * 1024 * 1024
AXES = ("row", "col")

ORDER = [0]
for far in range(1, Z // 2):
    ORDER += [Z - far, far]
ORDER.append(Z // 2)

PLANE = [[chip * CORES + core for chip in range(CHIPS)] for core in range(CORES)]
WHOLE = [
    [z * COLS + (z + k) % CHIPS * CORES + core for k in ORDER for core in range(CORES)] for z in range(Z)
]
SWAP = [(index, index ^ 1) for index in range(COLS)]
FORTH = [(z, (z + 1) % Z) for z in range(Z)]
BACK = [(z, (z - 1) % Z) for z in range(Z)]
LAST = (((1,), (1,)), ((), ()))


def gathered(value, axis, count):
    copies = jnp.broadcast_to(value[None], (count,) + value.shape)
    return lax.all_to_all(copies, axis, 0, 0)


def cost_kernel(core_ref, noise_ref, *refs, first, last, scale):
    size = noise_ref.shape[0]
    data_refs, refs = refs[:size], refs[size:]
    if not first:
        acc_ref, x_acc_ref, y_acc_ref, refs = refs[0], refs[3], refs[4], refs[5:]
    out_ref, keep_ref, sent_ref = refs[:3]
    low = core_ref[0] == 0
    half = noise_ref.shape[3]
    rows, columns = [], []
    xsq = ysq = 0.0
    if not first:
        xsq, ysq = x_acc_ref[...], y_acc_ref[...]
    for k in range(size):
        rows += [noise_ref[k, 0], noise_ref[k, 1]]
        chunk = data_refs[k][...]
        columns.append(chunk)
        left, right = chunk[:, :half], chunk[:, half:]
        keep_ref[k] = jnp.where(low, left, right)
        sent_ref[k] = jnp.where(low, right, left)
        xsq += rows[-2].astype(jnp.float32) ** 2 + rows[-1].astype(jnp.float32) ** 2
        ysq += left.astype(jnp.float32) ** 2 + right.astype(jnp.float32) ** 2
    rows = jnp.concatenate(rows, axis=1)
    columns = jnp.concatenate(columns, axis=1)
    total = lax.dot_general(rows, columns, LAST, preferred_element_type=jnp.float32)
    if not first:
        total += acc_ref[...]
    if last:
        xsq_column = jnp.sum(xsq, axis=1, keepdims=True)
        ysq_row = jnp.sum(ysq.T, axis=0, keepdims=True)
        total = (2.0 * total - xsq_column - ysq_row) * scale
        lanes = range(0, total.shape[1], half)
        top = functools.reduce(jnp.maximum, [total[:, k : k + half] for k in lanes])
        grown = jnp.exp(total - jnp.max(top, axis=1, keepdims=True))
        grown = functools.reduce(jnp.add, [grown[:, k : k + half] for k in lanes])
        refs[3][0:1, :] = jnp.max(top.T, axis=0, keepdims=True)
        refs[3][1:2, :] = jnp.sum(grown.T, axis=0, keepdims=True)
    else:
        refs[3][...] = xsq
        refs[4][...] = ysq
    out_ref[...] = total


def cost_step(core, pairs, chunks, start, carry, scale):
    size = len(chunks)
    last = start + size == Z
    block = start // size
    total, _, rows, half = pairs.shape
    columns, width = chunks[0].shape
    first = carry is None
    part = pl.BlockSpec((size, CORES, rows, half), lambda i, core: (block, 0, 0, 0))
    part_d = pl.BlockSpec((size, columns, half), lambda i, core: (block, 0, 0))
    tile = pl.BlockSpec((rows, columns), lambda i, core: (0, 0))
    narrow = pl.BlockSpec((rows, half), lambda i, core: (0, 0))
    whole = pl.BlockSpec(memory_space=pl.ANY)
    in_specs = [part] + [pl.BlockSpec((columns, width), lambda i, core: (0, 0))] * size
    args = [core, pairs, *chunks]
    aliases = {}
    if not first:
        aliases = {len(args) + k: k for k in ((1, 2) if last else range(5))}
        in_specs += [tile, whole, whole, narrow, narrow]
        args += list(carry)
    halves = jax.ShapeDtypeStruct((total, columns, half), jnp.bfloat16)
    stats = pl.BlockSpec((2, rows), lambda i, core: (0, 0))
    sums = [jax.ShapeDtypeStruct((rows, half), jnp.float32)] * 2
    if last:
        sums = [jax.ShapeDtypeStruct((2, rows), jnp.float32)]
    return pl.pallas_call(
        functools.partial(cost_kernel, first=first, last=last, scale=scale),
        grid_spec=pltpu.PrefetchScalarGridSpec(
            num_scalar_prefetch=1, grid=(1,), in_specs=in_specs, out_specs=[tile, part_d, part_d] + ([stats] if last else [narrow] * 2)
        ),
        out_shape=[jax.ShapeDtypeStruct((rows, columns), jnp.float32), halves, halves, *sums],
        input_output_aliases=aliases,
        compiler_params=pltpu.CompilerParams(
            dimension_semantics=("arbitrary",), vmem_limit_bytes=GRANT
        ),
        cost_estimate=pl.CostEstimate(
            flops=2 * rows * columns * width * size, bytes_accessed=6 * 1024 * 1024, transcendentals=0
        ),
        name="cost",
    )(*args)


def mix_kernel(z_ref, own_s_ref, other_s_ref, f_ref, g_ref, own_d_ref, other_d_ref, out_ref, plan, tail_ref):
    rows, columns = own_s_ref.shape
    count, half = out_ref.shape[0], out_ref.shape[2]
    step = pl.program_id(0)

    @pl.when(step == 0)
    def _():
        f = jnp.broadcast_to(f_ref[...], (8, rows)).T[:, :1]
        own = jnp.exp(own_s_ref[...] + f + g_ref[:1, :]).astype(jnp.bfloat16)
        other = jnp.exp(other_s_ref[...] + f + g_ref[1:2, :]).astype(jnp.bfloat16)
        plan[:, :columns] = own
        plan[:, columns:] = other
        ones = jnp.ones((EXTRA, columns), jnp.bfloat16)
        left = lax.dot_general(ones, own, LAST, preferred_element_type=jnp.float32)
        left += lax.dot_general(ones, other, LAST, preferred_element_type=jnp.float32)
        line = lax.broadcasted_iota(jnp.int32, (EXTRA, half), 0)
        tail = jnp.zeros((EXTRA, half), jnp.float32)
        pieces = rows // half
        for part in range(3):
            rounded = left.astype(jnp.bfloat16).astype(jnp.float32)
            left = left - rounded
            for k in range(pieces):
                tail = jnp.where(
                    line == part * pieces + k, rounded[:, k * half : (k + 1) * half], tail
                )
        tail_ref[...] = tail.astype(jnp.bfloat16)

    slots = []
    for k in range(count):
        chunk = lax.rem(step * count + k - z_ref[0] + Z, Z)
        slots.append(jnp.where(chunk < Z // 2, 2 * chunk, 2 * (Z - chunk) - 1))
    own_d = jnp.concatenate([own_d_ref[slot] for slot in slots], axis=1)
    other_d = jnp.concatenate([other_d_ref[slot] for slot in slots], axis=1)
    both = jnp.concatenate([own_d, other_d], axis=0)
    total = jnp.dot(plan[...], both, preferred_element_type=jnp.float32)
    for k in range(count):
        out_ref[k, :rows, :] = total[:, k * half : (k + 1) * half].astype(jnp.bfloat16)
        out_ref[k, rows:, :] = tail_ref[...]


def mixed(z, own_s, other_s, f, g, own_d, other_d):
    steps, columns, half = other_d.shape
    rows = own_s.shape[0]
    count = 4
    tile = pl.BlockSpec((rows, columns), lambda k, z: (0, 0))
    whole = pl.BlockSpec((steps, columns, half), lambda k, z: (0, 0, 0))
    return pl.pallas_call(
        mix_kernel,
        grid_spec=pltpu.PrefetchScalarGridSpec(
            num_scalar_prefetch=1,
            grid=(steps // count,),
            in_specs=[
                tile,
                tile,
                pl.BlockSpec((1, rows), lambda k, z: (0, 0)),
                pl.BlockSpec((2, columns), lambda k, z: (0, 0)),
                whole,
                whole,
            ],
            out_specs=pl.BlockSpec((count, rows + EXTRA, half), lambda k, z: (k, 0, 0)),
            scratch_shapes=[
                pltpu.VMEM((rows, 2 * columns), jnp.bfloat16),
                pltpu.VMEM((EXTRA, half), jnp.bfloat16),
            ],
        ),
        out_shape=jax.ShapeDtypeStruct((steps, rows + EXTRA, half), jnp.bfloat16),
        compiler_params=pltpu.CompilerParams(
            dimension_semantics=("arbitrary",), vmem_limit_bytes=GRANT // 2
        ),
        name="mix",
    )(z, own_s, other_s, f[None, :], g, own_d, other_d)


def shards(noise, data):
    n_row, n_col = lax.axis_size("row"), lax.axis_size("col")
    rows, half = noise.shape
    columns = data.shape[0]
    width = half * n_col
    core_word = jnp.full((1,), lax.rem(lax.axis_index("col"), CORES), jnp.int32)

    forth = back = data
    chunks = [data]
    for far in range(1, Z // 2 + 1):
        forth = lax.ppermute(forth, "row", FORTH)
        chunks.append(forth)
        if far < Z // 2:
            back = lax.ppermute(back, "row", BACK)
            chunks.append(back)
    ready, _ = lax.optimization_barrier((noise, chunks[1]))
    pairs = lax.all_to_all(
        jnp.broadcast_to(ready[None], (COLS,) + noise.shape), AXES, 0, 0, axis_index_groups=WHOLE
    ).reshape((CHIPS, CORES) + noise.shape)
    carry = None

    def cost(call):
        start, size = CALLS[call]
        now = chunks[start : start + size]
        return cost_step(core_word, pairs, now, start, carry, 1.0 / (width * blur))

    for call in range(len(CALLS)):
        carry = cost(call)
    scores, own_d, sent, stats = carry
    other_scores = lax.ppermute(scores, "col", SWAP)
    other_d = lax.ppermute(sent, "col", SWAP)

    shift = math.log(rows * n_row / (columns * n_col))
    tiles = (scores, other_scores)
    f = g = None
    for step in range(ITERS):
        if step == 0:
            pairs = gathered(stats, "col", n_col)
            top = jnp.max(pairs[:, 0], axis=0)
            f = -top - jnp.log(jnp.sum(pairs[:, 1] * jnp.exp(pairs[:, 0] - top), axis=0))
            tops, totals = [], []
            for tile in tiles:
                shifted = tile + f[:, None]
                tops.append(jnp.max(shifted, axis=0))
                totals.append(jnp.sum(jnp.exp(shifted - tops[-1][None, :]), axis=0))
            pairs = gathered(jnp.stack(tops + totals), "row", n_row)
            top = jnp.max(pairs[:, :CORES], axis=0)
            g = shift - top - jnp.log(jnp.sum(pairs[:, CORES:] * jnp.exp(pairs[:, :CORES] - top), axis=0))
            g, other_d = lax.optimization_barrier((g, other_d))
        else:
            total = jnp.sum(jnp.exp(scores + f[:, None] + g[0][None, :]), axis=1)
            f = f - jnp.log(jnp.sum(gathered(total[None], "col", n_col), axis=(0, 1)))
            totals = [
                jnp.sum(jnp.exp(tile + f[:, None] + g[k][None, :]), axis=0) for k, tile in enumerate(tiles)
            ]
            g = g + shift - jnp.log(jnp.sum(gathered(jnp.stack(totals), "row", n_row), axis=0))

    z_word = jnp.full((1,), lax.axis_index("row"), jnp.int32)
    pieces = mixed(z_word, scores, other_scores, f, g, own_d, other_d)
    f, g, pieces = lax.optimization_barrier((f * blur, g[0] * blur, pieces))
    landed = lax.all_to_all(pieces, "col", 0, 0, axis_index_groups=PLANE)
    summed = jnp.sum(landed.astype(jnp.float32), axis=0)
    mass = jnp.sum(summed[rows:].reshape(-1)[: 3 * rows].reshape(3, rows), axis=0)
    target = (summed[:rows] / mass[:, None] - noise.astype(jnp.float32)).astype(jnp.bfloat16)
    return (target, f, g)


def solution(mesh):
    return jax.shard_map(
        shards,
        mesh=mesh,
        in_specs=(P("row", "col"), P("col", "row")),
        out_specs=(P("row", "col"), P("row"), P("col")),
        check_vma=False,
    )
```

```python
import functools
import math

import jax
import jax.numpy as jnp
from jax import lax
from jax.experimental import pallas as pl
from jax.experimental.pallas import tpu as pltpu
from jax.sharding import PartitionSpec as P

ITERS = 4
blur = 0.01
X, Y, CORES, Z = 4, 4, 2, 16
CHIPS = X * Y
COLS = CHIPS * CORES
EXTRA = 16
CALLS = [(0, 14), (14, 2)]
GRANT = 56 * 1024 * 1024
AXES = ("row", "col")

ORDER = [0]
for far in range(1, Z // 2):
    ORDER += [Z - far, far]
ORDER.append(Z // 2)

PLANE = [[chip * CORES + core for chip in range(CHIPS)] for core in range(CORES)]
WHOLE = [
    [z * COLS + (z + k) % CHIPS * CORES + core for k in ORDER for core in range(CORES)] for z in range(Z)
]
SWAP = [(index, index ^ 1) for index in range(COLS)]
FORTH = [(z, (z + 1) % Z) for z in range(Z)]
BACK = [(z, (z - 1) % Z) for z in range(Z)]
LAST = (((1,), (1,)), ((), ()))


def gathered(value, axis, count):
    copies = jnp.broadcast_to(value[None], (count,) + value.shape)
    return lax.all_to_all(copies, axis, 0, 0)


def copies_kernel(value_ref, out_ref, done):
    copies = [pltpu.make_async_copy(value_ref, out_ref.at[k], done.at[k]) for k in range(out_ref.shape[0])]
    for copy in copies:
        copy.start()
    for copy in copies:
        copy.wait()


def copied(value, count):
    return pl.pallas_call(
        copies_kernel,
        in_specs=[pl.BlockSpec(memory_space=pltpu.VMEM)],
        out_specs=pl.BlockSpec(memory_space=pl.ANY),
        out_shape=jax.ShapeDtypeStruct((count,) + value.shape, value.dtype),
        scratch_shapes=[pltpu.SemaphoreType.DMA((count,))],
        name="copies",
    )(value)


def cost_kernel(word_ref, noise_ref, *refs, first, last, scale):
    size = noise_ref.shape[0]
    data_refs, refs = refs[:size], refs[size:]
    if not first:
        acc_ref, x_acc_ref, y_acc_ref, refs = refs[0], refs[3], refs[4], refs[5:]
    out_ref, keep_ref, sent_ref = refs[:3]
    low = word_ref[0] == 0
    half = noise_ref.shape[3]
    rows, columns = [], []
    xsq = ysq = 0.0
    if not first:
        xsq, ysq = x_acc_ref[...], y_acc_ref[...]
    for k in range(size):
        rows += [noise_ref[k, 0], noise_ref[k, 1]]
        chunk = data_refs[k][...]
        columns.append(chunk)
        left, right = chunk[:, :half], chunk[:, half:]
        keep_ref[k] = jnp.where(low, left, right)
        sent_ref[k] = jnp.where(low, right, left)
        xsq += rows[-2].astype(jnp.float32) ** 2 + rows[-1].astype(jnp.float32) ** 2
        ysq += left.astype(jnp.float32) ** 2 + right.astype(jnp.float32) ** 2
    rows = jnp.concatenate(rows, axis=1)
    columns = jnp.concatenate(columns, axis=1)
    total = lax.dot_general(rows, columns, LAST, preferred_element_type=jnp.float32)
    if not first:
        total += acc_ref[...]
    if last:
        xsq_column = jnp.sum(xsq, axis=1, keepdims=True)
        ysq_row = jnp.sum(ysq.T, axis=0, keepdims=True)
        total = (2.0 * total - xsq_column - ysq_row) * scale
        lanes = range(0, total.shape[1], half)
        top = functools.reduce(jnp.maximum, [total[:, k : k + half] for k in lanes])
        grown = jnp.exp(total - jnp.max(top, axis=1, keepdims=True))
        grown = functools.reduce(jnp.add, [grown[:, k : k + half] for k in lanes])
        refs[3][0:1, :] = jnp.max(top.T, axis=0, keepdims=True)
        refs[3][1:2, :] = jnp.sum(grown.T, axis=0, keepdims=True)
    else:
        refs[3][...] = xsq
        refs[4][...] = ysq
    out_ref[...] = total


def cost_step(words, pairs, chunks, start, carry, scale):
    size = len(chunks)
    last = start + size == Z
    block = start // size
    total, _, rows, half = pairs.shape
    columns, width = chunks[0].shape
    first = carry is None
    part = pl.BlockSpec((size, CORES, rows, half), lambda i, words: (block, 0, 0, 0))
    part_d = pl.BlockSpec((size, columns, half), lambda i, words: (block, 0, 0))
    tile = pl.BlockSpec((rows, columns), lambda i, words: (0, 0))
    narrow = pl.BlockSpec((rows, half), lambda i, words: (0, 0))
    whole = pl.BlockSpec(memory_space=pl.ANY)
    in_specs = [part] + [pl.BlockSpec((columns, width), lambda i, words: (0, 0))] * size
    args = [words, pairs, *chunks]
    aliases = {}
    if not first:
        aliases = {len(args) + k: k for k in ((1, 2) if last else range(5))}
        in_specs += [tile, whole, whole, narrow, narrow]
        args += list(carry)
    halves = jax.ShapeDtypeStruct((total, columns, half), jnp.bfloat16)
    stats = pl.BlockSpec((2, rows), lambda i, words: (0, 0))
    sums = [jax.ShapeDtypeStruct((rows, half), jnp.float32)] * 2
    if last:
        sums = [jax.ShapeDtypeStruct((2, rows), jnp.float32)]
    return pl.pallas_call(
        functools.partial(cost_kernel, first=first, last=last, scale=scale),
        grid_spec=pltpu.PrefetchScalarGridSpec(
            num_scalar_prefetch=1, grid=(1,), in_specs=in_specs, out_specs=[tile, part_d, part_d] + ([stats] if last else [narrow] * 2)
        ),
        out_shape=[jax.ShapeDtypeStruct((rows, columns), jnp.float32), halves, halves, *sums],
        input_output_aliases=aliases,
        compiler_params=pltpu.CompilerParams(
            dimension_semantics=("arbitrary",), vmem_limit_bytes=GRANT
        ),
        cost_estimate=pl.CostEstimate(
            flops=2 * rows * columns * width * size, bytes_accessed=6 * 1024 * 1024, transcendentals=0
        ),
        name="cost",
    )(*args)


def mix_kernel(word_ref, own_s_ref, other_s_ref, f_ref, g_ref, own_d_ref, other_d_ref, out_ref, plan, tail_ref):
    rows, columns = own_s_ref.shape
    count, half = out_ref.shape[0], out_ref.shape[2]
    step = pl.program_id(0)

    @pl.when(step == 0)
    def _():
        f = jnp.broadcast_to(f_ref[...], (8, rows)).T[:, :1]
        own = jnp.exp(own_s_ref[...] + f + g_ref[:1, :]).astype(jnp.bfloat16)
        other = jnp.exp(other_s_ref[...] + f + g_ref[1:2, :]).astype(jnp.bfloat16)
        plan[:, :columns] = own
        plan[:, columns:] = other
        ones = jnp.ones((EXTRA, columns), jnp.bfloat16)
        left = lax.dot_general(ones, own, LAST, preferred_element_type=jnp.float32)
        left += lax.dot_general(ones, other, LAST, preferred_element_type=jnp.float32)
        line = lax.broadcasted_iota(jnp.int32, (EXTRA, half), 0)
        tail = jnp.zeros((EXTRA, half), jnp.float32)
        pieces = rows // half
        for part in range(3):
            rounded = left.astype(jnp.bfloat16).astype(jnp.float32)
            left = left - rounded
            for k in range(pieces):
                tail = jnp.where(
                    line == part * pieces + k, rounded[:, k * half : (k + 1) * half], tail
                )
        tail_ref[...] = tail.astype(jnp.bfloat16)

    slots = []
    for k in range(count):
        chunk = lax.rem(step * count + k - word_ref[1] + Z, Z)
        slots.append(jnp.where(chunk < Z // 2, 2 * chunk, 2 * (Z - chunk) - 1))
    own_d = jnp.concatenate([own_d_ref[slot] for slot in slots], axis=1)
    other_d = jnp.concatenate([other_d_ref[slot] for slot in slots], axis=1)
    both = jnp.concatenate([own_d, other_d], axis=0)
    total = jnp.dot(plan[...], both, preferred_element_type=jnp.float32)
    for k in range(count):
        out_ref[k, :rows, :] = total[:, k * half : (k + 1) * half].astype(jnp.bfloat16)
        out_ref[k, rows:, :] = tail_ref[...]


def mixed(words, own_s, other_s, f, g, own_d, other_d):
    steps, columns, half = other_d.shape
    rows = own_s.shape[0]
    count = 4
    tile = pl.BlockSpec((rows, columns), lambda k, words: (0, 0))
    whole = pl.BlockSpec((steps, columns, half), lambda k, words: (0, 0, 0))
    return pl.pallas_call(
        mix_kernel,
        grid_spec=pltpu.PrefetchScalarGridSpec(
            num_scalar_prefetch=1,
            grid=(steps // count,),
            in_specs=[
                tile,
                tile,
                pl.BlockSpec((1, rows), lambda k, words: (0, 0)),
                pl.BlockSpec((2, columns), lambda k, words: (0, 0)),
                whole,
                whole,
            ],
            out_specs=pl.BlockSpec((count, rows + EXTRA, half), lambda k, words: (k, 0, 0)),
            scratch_shapes=[
                pltpu.VMEM((rows, 2 * columns), jnp.bfloat16),
                pltpu.VMEM((EXTRA, half), jnp.bfloat16),
            ],
        ),
        out_shape=jax.ShapeDtypeStruct((steps, rows + EXTRA, half), jnp.bfloat16),
        compiler_params=pltpu.CompilerParams(
            dimension_semantics=("arbitrary",), vmem_limit_bytes=GRANT // 2
        ),
        name="mix",
    )(words, own_s, other_s, f[None, :], g, own_d, other_d)


def shards(noise, data):
    n_row, n_col = lax.axis_size("row"), lax.axis_size("col")
    rows, half = noise.shape
    columns = data.shape[0]
    width = half * n_col
    words = jnp.stack([lax.rem(lax.axis_index("col"), CORES), lax.axis_index("row")]).astype(jnp.int32)

    pairs = lax.all_to_all(
        copied(noise, COLS), AXES, 0, 0, axis_index_groups=WHOLE
    ).reshape((CHIPS, CORES) + noise.shape)
    forth = back = data
    chunks = [data]
    for far in range(1, Z // 2 + 1):
        forth = lax.ppermute(forth, "row", FORTH)
        chunks.append(forth)
        if far < Z // 2:
            back = lax.ppermute(back, "row", BACK)
            chunks.append(back)
    carry = None

    def cost(call):
        start, size = CALLS[call]
        now = chunks[start : start + size]
        return cost_step(words, pairs, now, start, carry, 1.0 / (width * blur))

    for call in range(len(CALLS)):
        carry = cost(call)
    scores, own_d, sent, stats = carry
    other_scores = lax.ppermute(scores, "col", SWAP)
    other_d = lax.ppermute(sent, "col", SWAP)

    shift = math.log(rows * n_row / (columns * n_col))
    tiles = (scores, other_scores)
    f = g = None
    for step in range(ITERS):
        if step == 0:
            pairs = gathered(stats, "col", n_col)
            top = jnp.max(pairs[:, 0], axis=0)
            f = -top - jnp.log(jnp.sum(pairs[:, 1] * jnp.exp(pairs[:, 0] - top), axis=0))
            tops, totals = [], []
            for tile in tiles:
                shifted = tile + f[:, None]
                tops.append(jnp.max(shifted, axis=0))
                totals.append(jnp.sum(jnp.exp(shifted - tops[-1][None, :]), axis=0))
            pairs = gathered(jnp.stack(tops + totals), "row", n_row)
            top = jnp.max(pairs[:, :CORES], axis=0)
            g = shift - top - jnp.log(jnp.sum(pairs[:, CORES:] * jnp.exp(pairs[:, :CORES] - top), axis=0))
            g, other_d = lax.optimization_barrier((g, other_d))
        else:
            total = jnp.sum(jnp.exp(scores + f[:, None] + g[0][None, :]), axis=1)
            f = f - jnp.log(jnp.sum(gathered(total[None], "col", n_col), axis=(0, 1)))
            totals = [
                jnp.sum(jnp.exp(tile + f[:, None] + g[k][None, :]), axis=0) for k, tile in enumerate(tiles)
            ]
            g = g + shift - jnp.log(jnp.sum(gathered(jnp.stack(totals), "row", n_row), axis=0))

    pieces = mixed(words, scores, other_scores, f, g, own_d, other_d)
    f, g, pieces = lax.optimization_barrier((f * blur, g[0] * blur, pieces))
    landed = lax.all_to_all(pieces, "col", 0, 0, axis_index_groups=PLANE)
    summed = jnp.sum(landed.astype(jnp.float32), axis=0)
    mass = jnp.sum(summed[rows:].reshape(-1)[: 3 * rows].reshape(3, rows), axis=0)
    target = (summed[:rows] / mass[:, None] - noise.astype(jnp.float32)).astype(jnp.bfloat16)
    return (target, f, g)


def solution(mesh):
    return jax.shard_map(
        shards,
        mesh=mesh,
        in_specs=(P("row", "col"), P("col", "row")),
        out_specs=(P("row", "col"), P("row"), P("col")),
        check_vma=False,
    )
```

```python
import functools
import math

import jax
import jax.numpy as jnp
from jax import lax
from jax.experimental import pallas as pl
from jax.experimental.pallas import tpu as pltpu
from jax.sharding import PartitionSpec as P

ITERS = 4
blur = 0.01
X, Y, CORES, Z = 4, 4, 2, 16
CHIPS = X * Y
COLS = CHIPS * CORES
EXTRA = 16
CALLS = [(0, 14), (14, 2)]
GRANT = 56 * 1024 * 1024
AXES = ("row", "col")

ORDER = [0]
for far in range(1, Z // 2):
    ORDER += [Z - far, far]
ORDER.append(Z // 2)

PLANE = [[chip * CORES + core for chip in range(CHIPS)] for core in range(CORES)]
WHOLE = [
    [z * COLS + (z + k) % CHIPS * CORES + core for k in ORDER for core in range(CORES)] for z in range(Z)
]
SWAP = [(index, index ^ 1) for index in range(COLS)]
FORTH = [(z, (z + 1) % Z) for z in range(Z)]
BACK = [(z, (z - 1) % Z) for z in range(Z)]
LAST = (((1,), (1,)), ((), ()))


def gathered(value, axis, count):
    copies = jnp.broadcast_to(value[None], (count,) + value.shape)
    return lax.all_to_all(copies, axis, 0, 0)


def copies_kernel(value_ref, out_ref, done):
    copies = [pltpu.make_async_copy(value_ref, out_ref.at[k], done.at[k]) for k in range(out_ref.shape[0])]
    for copy in copies:
        copy.start()
    for copy in copies:
        copy.wait()


def copied(value, count):
    return pl.pallas_call(
        copies_kernel,
        in_specs=[pl.BlockSpec(memory_space=pltpu.VMEM)],
        out_specs=pl.BlockSpec(memory_space=pl.ANY),
        out_shape=jax.ShapeDtypeStruct((count,) + value.shape, value.dtype),
        scratch_shapes=[pltpu.SemaphoreType.DMA((count,))],
        name="copies",
    )(value)


def cost_kernel(core_ref, z_ref, noise_ref, *refs, first, last, scale):
    size = noise_ref.shape[0]
    data_refs, refs = refs[:size], refs[size:]
    if not first:
        acc_ref, x_acc_ref, y_acc_ref, refs = refs[0], refs[3], refs[4], refs[5:]
    out_ref, keep_ref, sent_ref = refs[:3]
    low = core_ref[0] == 0
    half = noise_ref.shape[3]
    rows, columns = [], []
    xsq = ysq = 0.0
    if not first:
        xsq, ysq = x_acc_ref[...], y_acc_ref[...]
    for k in range(size):
        rows += [noise_ref[k, 0], noise_ref[k, 1]]
        chunk = data_refs[k][...]
        columns.append(chunk)
        left, right = chunk[:, :half], chunk[:, half:]
        keep_ref[k] = jnp.where(low, left, right)
        sent_ref[k] = jnp.where(low, right, left)
        xsq += rows[-2].astype(jnp.float32) ** 2 + rows[-1].astype(jnp.float32) ** 2
        ysq += left.astype(jnp.float32) ** 2 + right.astype(jnp.float32) ** 2
    rows = jnp.concatenate(rows, axis=1)
    columns = jnp.concatenate(columns, axis=1)
    total = lax.dot_general(rows, columns, LAST, preferred_element_type=jnp.float32)
    if not first:
        total += acc_ref[...]
    if last:
        xsq_column = jnp.sum(xsq, axis=1, keepdims=True)
        ysq_row = jnp.sum(ysq.T, axis=0, keepdims=True)
        total = (2.0 * total - xsq_column - ysq_row) * scale
        lanes = range(0, total.shape[1], half)
        top = functools.reduce(jnp.maximum, [total[:, k : k + half] for k in lanes])
        grown = jnp.exp(total - jnp.max(top, axis=1, keepdims=True))
        grown = functools.reduce(jnp.add, [grown[:, k : k + half] for k in lanes])
        refs[3][0:1, :] = jnp.max(top.T, axis=0, keepdims=True)
        refs[3][1:2, :] = jnp.sum(grown.T, axis=0, keepdims=True)
    else:
        refs[3][...] = xsq
        refs[4][...] = ysq
    out_ref[...] = total


def cost_step(words, pairs, chunks, start, carry, scale):
    size = len(chunks)
    last = start + size == Z
    block = start // size
    total, _, rows, half = pairs.shape
    columns, width = chunks[0].shape
    first = carry is None
    part = pl.BlockSpec((size, CORES, rows, half), lambda i, core, z: (block, 0, 0, 0))
    part_d = pl.BlockSpec((size, columns, half), lambda i, core, z: (block, 0, 0))
    tile = pl.BlockSpec((rows, columns), lambda i, core, z: (0, 0))
    narrow = pl.BlockSpec((rows, half), lambda i, core, z: (0, 0))
    whole = pl.BlockSpec(memory_space=pl.ANY)
    in_specs = [part] + [pl.BlockSpec((columns, width), lambda i, core, z: (0, 0))] * size
    args = [*words, pairs, *chunks]
    aliases = {}
    if not first:
        aliases = {len(args) + k: k for k in ((1, 2) if last else range(5))}
        in_specs += [tile, whole, whole, narrow, narrow]
        args += list(carry)
    halves = jax.ShapeDtypeStruct((total, columns, half), jnp.bfloat16)
    stats = pl.BlockSpec((2, rows), lambda i, core, z: (0, 0))
    sums = [jax.ShapeDtypeStruct((rows, half), jnp.float32)] * 2
    if last:
        sums = [jax.ShapeDtypeStruct((2, rows), jnp.float32)]
    return pl.pallas_call(
        functools.partial(cost_kernel, first=first, last=last, scale=scale),
        grid_spec=pltpu.PrefetchScalarGridSpec(
            num_scalar_prefetch=2, grid=(1,), in_specs=in_specs, out_specs=[tile, part_d, part_d] + ([stats] if last else [narrow] * 2)
        ),
        out_shape=[jax.ShapeDtypeStruct((rows, columns), jnp.float32), halves, halves, *sums],
        input_output_aliases=aliases,
        compiler_params=pltpu.CompilerParams(
            dimension_semantics=("arbitrary",), vmem_limit_bytes=GRANT
        ),
        cost_estimate=pl.CostEstimate(
            flops=2 * rows * columns * width * size, bytes_accessed=6 * 1024 * 1024, transcendentals=0
        ),
        name="cost",
    )(*args)


def mix_kernel(z_ref, own_w_ref, other_w_ref, own_d_ref, other_d_ref, out_ref, tail_ref):
    rows, columns = own_w_ref.shape
    count, half = out_ref.shape[0], out_ref.shape[2]
    step = pl.program_id(0)

    @pl.when(step == 0)
    def _():
        ones = jnp.ones((EXTRA, columns), jnp.bfloat16)
        left = lax.dot_general(ones, own_w_ref[...], LAST, preferred_element_type=jnp.float32)
        left += lax.dot_general(ones, other_w_ref[...], LAST, preferred_element_type=jnp.float32)
        line = lax.broadcasted_iota(jnp.int32, (EXTRA, half), 0)
        tail = jnp.zeros((EXTRA, half), jnp.float32)
        pieces = rows // half
        for part in range(3):
            rounded = left.astype(jnp.bfloat16).astype(jnp.float32)
            left = left - rounded
            for k in range(pieces):
                tail = jnp.where(
                    line == part * pieces + k, rounded[:, k * half : (k + 1) * half], tail
                )
        tail_ref[...] = tail.astype(jnp.bfloat16)

    slots = []
    for k in range(count):
        chunk = lax.rem(step * count + k - z_ref[0] + Z, Z)
        slots.append(jnp.where(chunk < Z // 2, 2 * chunk, 2 * (Z - chunk) - 1))
    own_d = jnp.concatenate([own_d_ref[slot] for slot in slots], axis=1)
    other_d = jnp.concatenate([other_d_ref[slot] for slot in slots], axis=1)
    plan = jnp.concatenate([own_w_ref[...], other_w_ref[...]], axis=1)
    total = jnp.dot(plan, jnp.concatenate([own_d, other_d], axis=0), preferred_element_type=jnp.float32)
    for k in range(count):
        out_ref[k, :rows, :] = total[:, k * half : (k + 1) * half].astype(jnp.bfloat16)
        out_ref[k, rows:, :] = tail_ref[...]


def mixed(z, own_w, other_w, own_d, other_d):
    steps, columns, half = other_d.shape
    rows = own_w.shape[0]
    count = 4
    tile = pl.BlockSpec((rows, columns), lambda k, z: (0, 0))
    whole = pl.BlockSpec((steps, columns, half), lambda k, z: (0, 0, 0))
    return pl.pallas_call(
        mix_kernel,
        grid_spec=pltpu.PrefetchScalarGridSpec(
            num_scalar_prefetch=1,
            grid=(steps // count,),
            in_specs=[tile, tile, whole, whole],
            out_specs=pl.BlockSpec((count, rows + EXTRA, half), lambda k, z: (k, 0, 0)),
            scratch_shapes=[pltpu.VMEM((EXTRA, half), jnp.bfloat16)],
        ),
        out_shape=jax.ShapeDtypeStruct((steps, rows + EXTRA, half), jnp.bfloat16),
        compiler_params=pltpu.CompilerParams(
            dimension_semantics=("arbitrary",), vmem_limit_bytes=GRANT // 2
        ),
        name="mix",
    )(z, own_w, other_w, own_d, other_d)


def shards(noise, data):
    n_row, n_col = lax.axis_size("row"), lax.axis_size("col")
    rows, half = noise.shape
    columns = data.shape[0]
    width = half * n_col
    core_word = jnp.full((1,), lax.rem(lax.axis_index("col"), CORES), jnp.int32)
    z_word = jnp.full((1,), lax.axis_index("row"), jnp.int32)
    pairs = lax.all_to_all(
        copied(noise, COLS), AXES, 0, 0, axis_index_groups=WHOLE
    ).reshape((CHIPS, CORES) + noise.shape)
    forth = back = data
    chunks = [data]
    for far in range(1, Z // 2 + 1):
        forth = lax.ppermute(forth, "row", FORTH)
        chunks.append(forth)
        if far < Z // 2:
            back = lax.ppermute(back, "row", BACK)
            chunks.append(back)
    carry = None

    def cost(call):
        start, size = CALLS[call]
        now = chunks[start : start + size]
        return cost_step((core_word, z_word), pairs, now, start, carry, 1.0 / (width * blur))

    for call in range(len(CALLS)):
        carry = cost(call)
    scores, own_d, sent, stats = carry
    other_d = lax.ppermute(sent, "col", SWAP)

    shift = math.log(rows * n_row / (columns * n_col))
    f = g = None
    for step in range(ITERS):
        if step == 0:
            pairs = gathered(stats, "col", n_col)
            top = jnp.max(pairs[:, 0], axis=0)
            f = -top - jnp.log(jnp.sum(pairs[:, 1] * jnp.exp(pairs[:, 0] - top), axis=0))
            shifted = scores + f[:, None]
            top = jnp.max(shifted, axis=0)
            total = jnp.sum(jnp.exp(shifted - top[None, :]), axis=0)
            pairs = gathered(jnp.stack([top, total]), "row", n_row)
            top = jnp.max(pairs[:, 0], axis=0)
            g = shift - top - jnp.log(jnp.sum(pairs[:, 1] * jnp.exp(pairs[:, 0] - top), axis=0))
        else:
            total = jnp.sum(jnp.exp(scores + f[:, None] + g[None, :]), axis=1)
            f = f - jnp.log(jnp.sum(gathered(total[None], "col", n_col), axis=(0, 1)))
            total = jnp.sum(jnp.exp(scores + f[:, None] + g[None, :]), axis=0)
            g = g + shift - jnp.log(jnp.sum(gathered(total[None], "row", n_row), axis=(0, 1)))

    own_w = jnp.exp(scores + f[:, None] + g[None, :]).astype(jnp.bfloat16)
    other_w = lax.ppermute(own_w, "col", SWAP)
    pieces = mixed(z_word, own_w, other_w, own_d, other_d)
    f, g, pieces = lax.optimization_barrier((f * blur, g * blur, pieces))
    landed = lax.all_to_all(pieces, "col", 0, 0, axis_index_groups=PLANE)
    summed = jnp.sum(landed.astype(jnp.float32), axis=0)
    mass = jnp.sum(summed[rows:].reshape(-1)[: 3 * rows].reshape(3, rows), axis=0)
    target = (summed[:rows] / mass[:, None] - noise.astype(jnp.float32)).astype(jnp.bfloat16)
    return (target, f, g)


def solution(mesh):
    return jax.shard_map(
        shards,
        mesh=mesh,
        in_specs=(P("row", "col"), P("col", "row")),
        out_specs=(P("row", "col"), P("row"), P("col")),
        check_vma=False,
    )
```

```python
import functools
import math

import jax
import jax.numpy as jnp
from jax import lax
from jax.experimental import pallas as pl
from jax.experimental.pallas import tpu as pltpu
from jax.sharding import PartitionSpec as P

ITERS = 4
blur = 0.01
X, Y, CORES, Z = 4, 4, 2, 16
CHIPS = X * Y
COLS = CHIPS * CORES
EXTRA = 16
CALLS = [(0, 14), (14, 2)]
COST_GRANT = 48 * 1024 * 1024
MIX_GRANT = 28 * 1024 * 1024
AXES = ("row", "col")

ORDER = [0]
for far in range(1, Z // 2):
    ORDER += [Z - far, far]
ORDER.append(Z // 2)

PLANE = [[chip * CORES + core for chip in range(CHIPS)] for core in range(CORES)]
WHOLE = [
    [z * COLS + (z + k) % CHIPS * CORES + core for k in ORDER for core in range(CORES)] for z in range(Z)
]
SWAP = [(index, index ^ 1) for index in range(COLS)]
FORTH = [(z, (z + 1) % Z) for z in range(Z)]
BACK = [(z, (z - 1) % Z) for z in range(Z)]
LAST = (((1,), (1,)), ((), ()))


def gathered(value, axis, count):
    copies = jnp.broadcast_to(value[None], (count,) + value.shape)
    return lax.all_to_all(copies, axis, 0, 0)


def copies_kernel(value_ref, out_ref, done):
    copies = [pltpu.make_async_copy(value_ref, out_ref.at[k], done.at[k]) for k in range(out_ref.shape[0])]
    for copy in copies:
        copy.start()
    for copy in copies:
        copy.wait()


def copied(value, count):
    return pl.pallas_call(
        copies_kernel,
        in_specs=[pl.BlockSpec(memory_space=pltpu.VMEM)],
        out_specs=pl.BlockSpec(memory_space=pl.ANY),
        out_shape=jax.ShapeDtypeStruct((count,) + value.shape, value.dtype),
        scratch_shapes=[pltpu.SemaphoreType.DMA((count,))],
        name="copies",
    )(value)


def cost_kernel(core_ref, z_ref, noise_ref, *refs, first, last, scale):
    size = noise_ref.shape[0]
    data_refs, refs = refs[:size], refs[size:]
    if not first:
        acc_ref, x_acc_ref, y_acc_ref, refs = refs[0], refs[3], refs[4], refs[5:]
    out_ref, keep_ref, sent_ref = refs[:3]
    low = core_ref[0] == 0
    half = noise_ref.shape[3]
    rows, columns = [], []
    xsq = ysq = 0.0
    if not first:
        xsq, ysq = x_acc_ref[...], y_acc_ref[...]
    for k in range(size):
        rows += [noise_ref[k, 0], noise_ref[k, 1]]
        chunk = data_refs[k][...]
        columns.append(chunk)
        left, right = chunk[:, :half], chunk[:, half:]
        keep_ref[k] = jnp.where(low, left, right)
        sent_ref[k] = jnp.where(low, right, left)
        xsq += rows[-2].astype(jnp.float32) ** 2 + rows[-1].astype(jnp.float32) ** 2
        ysq += left.astype(jnp.float32) ** 2 + right.astype(jnp.float32) ** 2
    rows = jnp.concatenate(rows, axis=1)
    columns = jnp.concatenate(columns, axis=1)
    total = lax.dot_general(rows, columns, LAST, preferred_element_type=jnp.float32)
    if not first:
        total += acc_ref[...]
    if last:
        xsq_column = jnp.sum(xsq, axis=1, keepdims=True)
        ysq_row = jnp.sum(ysq.T, axis=0, keepdims=True)
        total = (2.0 * total - xsq_column - ysq_row) * scale
        lanes = range(0, total.shape[1], half)
        top = functools.reduce(jnp.maximum, [total[:, k : k + half] for k in lanes])
        grown = jnp.exp(total - jnp.max(top, axis=1, keepdims=True))
        grown = functools.reduce(jnp.add, [grown[:, k : k + half] for k in lanes])
        refs[3][0:1, :] = jnp.max(top.T, axis=0, keepdims=True)
        refs[3][1:2, :] = jnp.sum(grown.T, axis=0, keepdims=True)
    else:
        refs[3][...] = xsq
        refs[4][...] = ysq
    out_ref[...] = total


def cost_step(words, pairs, chunks, start, carry, scale):
    size = len(chunks)
    last = start + size == Z
    block = start // size
    total, _, rows, half = pairs.shape
    columns, width = chunks[0].shape
    first = carry is None
    part = pl.BlockSpec((size, CORES, rows, half), lambda i, core, z: (block, 0, 0, 0))
    part_d = pl.BlockSpec((size, columns, half), lambda i, core, z: (block, 0, 0))
    tile = pl.BlockSpec((rows, columns), lambda i, core, z: (0, 0))
    narrow = pl.BlockSpec((rows, half), lambda i, core, z: (0, 0))
    whole = pl.BlockSpec(memory_space=pl.ANY)
    in_specs = [part] + [pl.BlockSpec((columns, width), lambda i, core, z: (0, 0))] * size
    args = [*words, pairs, *chunks]
    aliases = {}
    if not first:
        aliases = {len(args) + k: k for k in ((1, 2) if last else range(5))}
        in_specs += [tile, whole, whole, narrow, narrow]
        args += list(carry)
    halves = jax.ShapeDtypeStruct((total, columns, half), jnp.bfloat16)
    stats = pl.BlockSpec((2, rows), lambda i, core, z: (0, 0))
    sums = [jax.ShapeDtypeStruct((rows, half), jnp.float32)] * 2
    if last:
        sums = [jax.ShapeDtypeStruct((2, rows), jnp.float32)]
    return pl.pallas_call(
        functools.partial(cost_kernel, first=first, last=last, scale=scale),
        grid_spec=pltpu.PrefetchScalarGridSpec(
            num_scalar_prefetch=2, grid=(1,), in_specs=in_specs, out_specs=[tile, part_d, part_d] + ([stats] if last else [narrow] * 2)
        ),
        out_shape=[jax.ShapeDtypeStruct((rows, columns), jnp.float32), halves, halves, *sums],
        input_output_aliases=aliases,
        compiler_params=pltpu.CompilerParams(
            dimension_semantics=("arbitrary",), vmem_limit_bytes=COST_GRANT
        ),
        cost_estimate=pl.CostEstimate(
            flops=2 * rows * columns * width * size, bytes_accessed=6 * 1024 * 1024, transcendentals=0
        ),
        name="cost",
    )(*args)


def mix_kernel(z_ref, own_w_ref, other_w_ref, own_d_ref, other_d_ref, out_ref, tail_ref):
    rows, columns = own_w_ref.shape
    count, half = out_ref.shape[0], out_ref.shape[2]
    step = pl.program_id(0)

    @pl.when(step == 0)
    def _():
        ones = jnp.ones((EXTRA, columns), jnp.bfloat16)
        left = lax.dot_general(ones, own_w_ref[...], LAST, preferred_element_type=jnp.float32)
        left += lax.dot_general(ones, other_w_ref[...], LAST, preferred_element_type=jnp.float32)
        line = lax.broadcasted_iota(jnp.int32, (EXTRA, half), 0)
        tail = jnp.zeros((EXTRA, half), jnp.float32)
        pieces = rows // half
        for part in range(3):
            rounded = left.astype(jnp.bfloat16).astype(jnp.float32)
            left = left - rounded
            for k in range(pieces):
                tail = jnp.where(
                    line == part * pieces + k, rounded[:, k * half : (k + 1) * half], tail
                )
        tail_ref[...] = tail.astype(jnp.bfloat16)

    slots = []
    for k in range(count):
        chunk = lax.rem(step * count + k - z_ref[0] + Z, Z)
        slots.append(jnp.where(chunk < Z // 2, 2 * chunk, 2 * (Z - chunk) - 1))
    own_d = jnp.concatenate([own_d_ref[slot] for slot in slots], axis=1)
    other_d = jnp.concatenate([other_d_ref[slot] for slot in slots], axis=1)
    plan = jnp.concatenate([own_w_ref[...], other_w_ref[...]], axis=1)
    total = jnp.dot(plan, jnp.concatenate([own_d, other_d], axis=0), preferred_element_type=jnp.float32)
    for k in range(count):
        out_ref[k, :rows, :] = total[:, k * half : (k + 1) * half].astype(jnp.bfloat16)
        out_ref[k, rows:, :] = tail_ref[...]


def mixed(z, own_w, other_w, own_d, other_d):
    steps, columns, half = other_d.shape
    rows = own_w.shape[0]
    count = 4
    tile = pl.BlockSpec((rows, columns), lambda k, z: (0, 0))
    whole = pl.BlockSpec((steps, columns, half), lambda k, z: (0, 0, 0))
    return pl.pallas_call(
        mix_kernel,
        grid_spec=pltpu.PrefetchScalarGridSpec(
            num_scalar_prefetch=1,
            grid=(steps // count,),
            in_specs=[tile, tile, whole, whole],
            out_specs=pl.BlockSpec((count, rows + EXTRA, half), lambda k, z: (k, 0, 0)),
            scratch_shapes=[pltpu.VMEM((EXTRA, half), jnp.bfloat16)],
        ),
        out_shape=jax.ShapeDtypeStruct((steps, rows + EXTRA, half), jnp.bfloat16),
        compiler_params=pltpu.CompilerParams(
            dimension_semantics=("arbitrary",), vmem_limit_bytes=MIX_GRANT
        ),
        name="mix",
    )(z, own_w, other_w, own_d, other_d)


def shards(noise, data):
    n_row, n_col = lax.axis_size("row"), lax.axis_size("col")
    rows, half = noise.shape
    columns = data.shape[0]
    width = half * n_col
    core_word = jnp.full((1,), lax.rem(lax.axis_index("col"), CORES), jnp.int32)
    z_word = jnp.full((1,), lax.axis_index("row"), jnp.int32)
    pairs = lax.all_to_all(
        copied(noise, COLS), AXES, 0, 0, axis_index_groups=WHOLE
    ).reshape((CHIPS, CORES) + noise.shape)
    forth = back = data
    chunks = [data]
    for far in range(1, Z // 2 + 1):
        forth = lax.ppermute(forth, "row", FORTH)
        chunks.append(forth)
        if far < Z // 2:
            back = lax.ppermute(back, "row", BACK)
            chunks.append(back)
    carry = None

    def cost(call):
        start, size = CALLS[call]
        now = chunks[start : start + size]
        return cost_step((core_word, z_word), pairs, now, start, carry, 1.0 / (width * blur))

    for call in range(len(CALLS)):
        carry = cost(call)
    scores, own_d, sent, stats = carry
    other_d = lax.ppermute(sent, "col", SWAP)

    shift = math.log(rows * n_row / (columns * n_col))
    f = g = None
    for step in range(ITERS):
        if step == 0:
            pairs = gathered(stats, "col", n_col)
            top = jnp.max(pairs[:, 0], axis=0)
            f = -top - jnp.log(jnp.sum(pairs[:, 1] * jnp.exp(pairs[:, 0] - top), axis=0))
            shifted = scores + f[:, None]
            top = jnp.max(shifted, axis=0)
            total = jnp.sum(jnp.exp(shifted - top[None, :]), axis=0)
            pairs = gathered(jnp.stack([top, total]), "row", n_row)
            top = jnp.max(pairs[:, 0], axis=0)
            g = shift - top - jnp.log(jnp.sum(pairs[:, 1] * jnp.exp(pairs[:, 0] - top), axis=0))
        else:
            total = jnp.sum(jnp.exp(scores + f[:, None] + g[None, :]), axis=1)
            f = f - jnp.log(jnp.sum(gathered(total[None], "col", n_col), axis=(0, 1)))
            total = jnp.sum(jnp.exp(scores + f[:, None] + g[None, :]), axis=0)
            g = g + shift - jnp.log(jnp.sum(gathered(total[None], "row", n_row), axis=(0, 1)))

    own_w = jnp.exp(scores + f[:, None] + g[None, :]).astype(jnp.bfloat16)
    other_w = lax.ppermute(own_w, "col", SWAP)
    pieces = mixed(z_word, own_w, other_w, own_d, other_d)
    f, g, pieces = lax.optimization_barrier((f * blur, g * blur, pieces))
    landed = lax.all_to_all(pieces, "col", 0, 0, axis_index_groups=PLANE)
    summed = jnp.sum(landed.astype(jnp.float32), axis=0)
    mass = jnp.sum(summed[rows:].reshape(-1)[: 3 * rows].reshape(3, rows), axis=0)
    target = (summed[:rows] / mass[:, None] - noise.astype(jnp.float32)).astype(jnp.bfloat16)
    return (target, f, g)


def solution(mesh):
    return jax.shard_map(
        shards,
        mesh=mesh,
        in_specs=(P("row", "col"), P("col", "row")),
        out_specs=(P("row", "col"), P("row"), P("col")),
        check_vma=False,
    )
```

```python
import functools
import math

import jax
import jax.numpy as jnp
from jax import lax
from jax.experimental import pallas as pl
from jax.experimental.pallas import tpu as pltpu
from jax.sharding import PartitionSpec as P

ITERS = 4
blur = 0.01
X, Y, CORES, Z = 4, 4, 2, 16
CHIPS = X * Y
COLS = CHIPS * CORES
EXTRA = 16
CALLS = [(0, 14), (14, 2)]
COST_GRANTS = (48 * 1024 * 1024, 50 * 1024 * 1024)
MIX_GRANT = 28 * 1024 * 1024
AXES = ("row", "col")

ORDER = [0]
for far in range(1, Z // 2):
    ORDER += [Z - far, far]
ORDER.append(Z // 2)

PLANE = [[chip * CORES + core for chip in range(CHIPS)] for core in range(CORES)]
WHOLE = [
    [z * COLS + (z + k) % CHIPS * CORES + core for k in ORDER for core in range(CORES)] for z in range(Z)
]
SWAP = [(index, index ^ 1) for index in range(COLS)]
FORTH = [(z, (z + 1) % Z) for z in range(Z)]
BACK = [(z, (z - 1) % Z) for z in range(Z)]
LAST = (((1,), (1,)), ((), ()))


def gathered(value, axis, count):
    copies = jnp.broadcast_to(value[None], (count,) + value.shape)
    return lax.all_to_all(copies, axis, 0, 0)


def copies_kernel(value_ref, out_ref, done):
    copies = [pltpu.make_async_copy(value_ref, out_ref.at[k], done.at[k]) for k in range(out_ref.shape[0])]
    for copy in copies:
        copy.start()
    for copy in copies:
        copy.wait()


def copied(value, count):
    return pl.pallas_call(
        copies_kernel,
        in_specs=[pl.BlockSpec(memory_space=pltpu.VMEM)],
        out_specs=pl.BlockSpec(memory_space=pl.ANY),
        out_shape=jax.ShapeDtypeStruct((count,) + value.shape, value.dtype),
        scratch_shapes=[pltpu.SemaphoreType.DMA((count,))],
        name="copies",
    )(value)


def cost_kernel(core_ref, z_ref, noise_ref, *refs, first, last, scale):
    size = noise_ref.shape[0]
    data_refs, refs = refs[:size], refs[size:]
    if not first:
        acc_ref, x_acc_ref, y_acc_ref, refs = refs[0], refs[3], refs[4], refs[5:]
    out_ref, keep_ref, sent_ref = refs[:3]
    low = core_ref[0] == 0
    half = noise_ref.shape[3]
    rows, columns = [], []
    xsq = ysq = 0.0
    if not first:
        xsq, ysq = x_acc_ref[...], y_acc_ref[...]
    for k in range(size):
        rows += [noise_ref[k, 0], noise_ref[k, 1]]
        chunk = data_refs[k][...]
        columns.append(chunk)
        left, right = chunk[:, :half], chunk[:, half:]
        keep_ref[k] = jnp.where(low, left, right)
        sent_ref[k] = jnp.where(low, right, left)
        xsq += rows[-2].astype(jnp.float32) ** 2 + rows[-1].astype(jnp.float32) ** 2
        ysq += left.astype(jnp.float32) ** 2 + right.astype(jnp.float32) ** 2
    rows = jnp.concatenate(rows, axis=1)
    columns = jnp.concatenate(columns, axis=1)
    total = lax.dot_general(rows, columns, LAST, preferred_element_type=jnp.float32)
    if not first:
        total += acc_ref[...]
    if last:
        xsq_column = jnp.sum(xsq, axis=1, keepdims=True)
        ysq_row = jnp.sum(ysq.T, axis=0, keepdims=True)
        total = (2.0 * total - xsq_column - ysq_row) * scale
        lanes = range(0, total.shape[1], half)
        top = functools.reduce(jnp.maximum, [total[:, k : k + half] for k in lanes])
        grown = jnp.exp(total - jnp.max(top, axis=1, keepdims=True))
        grown = functools.reduce(jnp.add, [grown[:, k : k + half] for k in lanes])
        refs[3][0:1, :] = jnp.max(top.T, axis=0, keepdims=True)
        refs[3][1:2, :] = jnp.sum(grown.T, axis=0, keepdims=True)
    else:
        refs[3][...] = xsq
        refs[4][...] = ysq
    out_ref[...] = total


def cost_step(words, pairs, chunks, start, carry, scale):
    size = len(chunks)
    last = start + size == Z
    block = start // size
    total, _, rows, half = pairs.shape
    columns, width = chunks[0].shape
    first = carry is None
    part = pl.BlockSpec((size, CORES, rows, half), lambda i, core, z: (block, 0, 0, 0))
    part_d = pl.BlockSpec((size, columns, half), lambda i, core, z: (block, 0, 0))
    tile = pl.BlockSpec((rows, columns), lambda i, core, z: (0, 0))
    narrow = pl.BlockSpec((rows, half), lambda i, core, z: (0, 0))
    whole = pl.BlockSpec(memory_space=pl.ANY)
    in_specs = [part] + [pl.BlockSpec((columns, width), lambda i, core, z: (0, 0))] * size
    args = [*words, pairs, *chunks]
    aliases = {}
    if not first:
        aliases = {len(args) + k: k for k in ((1, 2) if last else range(5))}
        in_specs += [tile, whole, whole, narrow, narrow]
        args += list(carry)
    halves = jax.ShapeDtypeStruct((total, columns, half), jnp.bfloat16)
    stats = pl.BlockSpec((2, rows), lambda i, core, z: (0, 0))
    sums = [jax.ShapeDtypeStruct((rows, half), jnp.float32)] * 2
    if last:
        sums = [jax.ShapeDtypeStruct((2, rows), jnp.float32)]
    return pl.pallas_call(
        functools.partial(cost_kernel, first=first, last=last, scale=scale),
        grid_spec=pltpu.PrefetchScalarGridSpec(
            num_scalar_prefetch=2, grid=(1,), in_specs=in_specs, out_specs=[tile, part_d, part_d] + ([stats] if last else [narrow] * 2)
        ),
        out_shape=[jax.ShapeDtypeStruct((rows, columns), jnp.float32), halves, halves, *sums],
        input_output_aliases=aliases,
        compiler_params=pltpu.CompilerParams(
            dimension_semantics=("arbitrary",), vmem_limit_bytes=COST_GRANTS[last]
        ),
        cost_estimate=pl.CostEstimate(
            flops=2 * rows * columns * width * size, bytes_accessed=6 * 1024 * 1024, transcendentals=0
        ),
        name="cost",
    )(*args)


def mix_kernel(z_ref, own_w_ref, other_w_ref, own_d_ref, other_d_ref, out_ref, tail_ref):
    rows, columns = own_w_ref.shape
    count, half = out_ref.shape[0], out_ref.shape[2]
    step = pl.program_id(0)

    @pl.when(step == 0)
    def _():
        ones = jnp.ones((EXTRA, columns), jnp.bfloat16)
        left = lax.dot_general(ones, own_w_ref[...], LAST, preferred_element_type=jnp.float32)
        left += lax.dot_general(ones, other_w_ref[...], LAST, preferred_element_type=jnp.float32)
        line = lax.broadcasted_iota(jnp.int32, (EXTRA, half), 0)
        tail = jnp.zeros((EXTRA, half), jnp.float32)
        pieces = rows // half
        for part in range(3):
            rounded = left.astype(jnp.bfloat16).astype(jnp.float32)
            left = left - rounded
            for k in range(pieces):
                tail = jnp.where(
                    line == part * pieces + k, rounded[:, k * half : (k + 1) * half], tail
                )
        tail_ref[...] = tail.astype(jnp.bfloat16)

    slots = []
    for k in range(count):
        chunk = lax.rem(step * count + k - z_ref[0] + Z, Z)
        slots.append(jnp.where(chunk < Z // 2, 2 * chunk, 2 * (Z - chunk) - 1))
    own_d = jnp.concatenate([own_d_ref[slot] for slot in slots], axis=1)
    other_d = jnp.concatenate([other_d_ref[slot] for slot in slots], axis=1)
    plan = jnp.concatenate([own_w_ref[...], other_w_ref[...]], axis=1)
    total = jnp.dot(plan, jnp.concatenate([own_d, other_d], axis=0), preferred_element_type=jnp.float32)
    for k in range(count):
        out_ref[k, :rows, :] = total[:, k * half : (k + 1) * half].astype(jnp.bfloat16)
        out_ref[k, rows:, :] = tail_ref[...]


def mixed(z, own_w, other_w, own_d, other_d):
    steps, columns, half = other_d.shape
    rows = own_w.shape[0]
    count = 4
    tile = pl.BlockSpec((rows, columns), lambda k, z: (0, 0))
    whole = pl.BlockSpec((steps, columns, half), lambda k, z: (0, 0, 0))
    return pl.pallas_call(
        mix_kernel,
        grid_spec=pltpu.PrefetchScalarGridSpec(
            num_scalar_prefetch=1,
            grid=(steps // count,),
            in_specs=[tile, tile, whole, whole],
            out_specs=pl.BlockSpec((count, rows + EXTRA, half), lambda k, z: (k, 0, 0)),
            scratch_shapes=[pltpu.VMEM((EXTRA, half), jnp.bfloat16)],
        ),
        out_shape=jax.ShapeDtypeStruct((steps, rows + EXTRA, half), jnp.bfloat16),
        compiler_params=pltpu.CompilerParams(
            dimension_semantics=("arbitrary",), vmem_limit_bytes=MIX_GRANT
        ),
        name="mix",
    )(z, own_w, other_w, own_d, other_d)


def shards(noise, data):
    n_row, n_col = lax.axis_size("row"), lax.axis_size("col")
    rows, half = noise.shape
    columns = data.shape[0]
    width = half * n_col
    core_word = jnp.full((1,), lax.rem(lax.axis_index("col"), CORES), jnp.int32)
    z_word = jnp.full((1,), lax.axis_index("row"), jnp.int32)
    pairs = lax.all_to_all(
        copied(noise, COLS), AXES, 0, 0, axis_index_groups=WHOLE
    ).reshape((CHIPS, CORES) + noise.shape)
    forth = back = data
    chunks = [data]
    for far in range(1, Z // 2 + 1):
        forth = lax.ppermute(forth, "row", FORTH)
        chunks.append(forth)
        if far < Z // 2:
            back = lax.ppermute(back, "row", BACK)
            chunks.append(back)
    carry = None

    def cost(call):
        start, size = CALLS[call]
        now = chunks[start : start + size]
        return cost_step((core_word, z_word), pairs, now, start, carry, 1.0 / (width * blur))

    for call in range(len(CALLS)):
        carry = cost(call)
    scores, own_d, sent, stats = carry
    other_d = lax.ppermute(sent, "col", SWAP)

    shift = math.log(rows * n_row / (columns * n_col))
    f = g = None
    for step in range(ITERS):
        if step == 0:
            pairs = gathered(stats, "col", n_col)
            top = jnp.max(pairs[:, 0], axis=0)
            f = -top - jnp.log(jnp.sum(pairs[:, 1] * jnp.exp(pairs[:, 0] - top), axis=0))
            shifted = scores + f[:, None]
            top = jnp.max(shifted, axis=0)
            total = jnp.sum(jnp.exp(shifted - top[None, :]), axis=0)
            pairs = gathered(jnp.stack([top, total]), "row", n_row)
            top = jnp.max(pairs[:, 0], axis=0)
            g = shift - top - jnp.log(jnp.sum(pairs[:, 1] * jnp.exp(pairs[:, 0] - top), axis=0))
        else:
            total = jnp.sum(jnp.exp(scores + f[:, None] + g[None, :]), axis=1)
            f = f - jnp.log(jnp.sum(gathered(total[None], "col", n_col), axis=(0, 1)))
            total = jnp.sum(jnp.exp(scores + f[:, None] + g[None, :]), axis=0)
            g = g + shift - jnp.log(jnp.sum(gathered(total[None], "row", n_row), axis=(0, 1)))

    own_w = jnp.exp(scores + f[:, None] + g[None, :]).astype(jnp.bfloat16)
    other_w = lax.ppermute(own_w, "col", SWAP)
    pieces = mixed(z_word, own_w, other_w, own_d, other_d)
    f, g, pieces = lax.optimization_barrier((f * blur, g * blur, pieces))
    landed = lax.all_to_all(pieces, "col", 0, 0, axis_index_groups=PLANE)
    summed = jnp.sum(landed.astype(jnp.float32), axis=0)
    mass = jnp.sum(summed[rows:].reshape(-1)[: 3 * rows].reshape(3, rows), axis=0)
    target = (summed[:rows] / mass[:, None] - noise.astype(jnp.float32)).astype(jnp.bfloat16)
    return (target, f, g)


def solution(mesh):
    return jax.shard_map(
        shards,
        mesh=mesh,
        in_specs=(P("row", "col"), P("col", "row")),
        out_specs=(P("row", "col"), P("row"), P("col")),
        check_vma=False,
    )
```

```python
import functools
import math

import jax
import jax.numpy as jnp
from jax import lax
from jax.experimental import pallas as pl
from jax.experimental.pallas import tpu as pltpu
from jax.sharding import PartitionSpec as P

ITERS = 4
blur = 0.01
X, Y, CORES, Z = 4, 4, 2, 16
CHIPS = X * Y
COLS = CHIPS * CORES
EXTRA = 16
CALLS = [(0, 15), (15, 1)]
COST_GRANTS = (48 * 1024 * 1024, 50 * 1024 * 1024)
MIX_GRANT = 28 * 1024 * 1024
AXES = ("row", "col")

ORDER = [0]
for far in range(1, Z // 2):
    ORDER += [Z - far, far]
ORDER.append(Z // 2)

PLANE = [[chip * CORES + core for chip in range(CHIPS)] for core in range(CORES)]
WHOLE = [
    [z * COLS + (z + k) % CHIPS * CORES + core for k in ORDER for core in range(CORES)] for z in range(Z)
]
SWAP = [(index, index ^ 1) for index in range(COLS)]
FORTH = [
    (z * COLS + col, (z + (1 if col % CORES == 0 else -1)) % Z * COLS + col) for z in range(Z) for col in range(COLS)
]
BACK = [(to, start) for start, to in FORTH]
LAST = (((1,), (1,)), ((), ()))


def gathered(value, axis, count):
    copies = jnp.broadcast_to(value[None], (count,) + value.shape)
    return lax.all_to_all(copies, axis, 0, 0)


def copies_kernel(value_ref, out_ref, done):
    copies = [pltpu.make_async_copy(value_ref, out_ref.at[k], done.at[k]) for k in range(out_ref.shape[0])]
    for copy in copies:
        copy.start()
    for copy in copies:
        copy.wait()


def copied(value, count):
    return pl.pallas_call(
        copies_kernel,
        in_specs=[pl.BlockSpec(memory_space=pltpu.VMEM)],
        out_specs=pl.BlockSpec(memory_space=pl.ANY),
        out_shape=jax.ShapeDtypeStruct((count,) + value.shape, value.dtype),
        scratch_shapes=[pltpu.SemaphoreType.DMA((count,))],
        name="copies",
    )(value)


def cost_kernel(core_ref, z_ref, noise_ref, *refs, first, last, scale):
    size = noise_ref.shape[0]
    data_refs, refs = refs[:size], refs[size:]
    if not first:
        acc_ref, x_acc_ref, y_acc_ref, refs = refs[0], refs[3], refs[4], refs[5:]
    out_ref, keep_ref, sent_ref = refs[:3]
    low = core_ref[0] == 0
    half = noise_ref.shape[3]
    rows, columns = [], []
    xsq = ysq = 0.0
    if not first:
        xsq, ysq = x_acc_ref[...], y_acc_ref[...]
    for k in range(size):
        turned = 0 if k == 0 or size == 1 else (1 if k % 2 else -1)
        slot = k + turned * core_ref[0]
        rows += [noise_ref[slot, 0], noise_ref[slot, 1]]
        chunk = data_refs[k][...]
        columns.append(chunk)
        left, right = chunk[:, :half], chunk[:, half:]
        keep_ref[k] = jnp.where(low, left, right)
        sent_ref[k] = jnp.where(low, right, left)
        xsq += rows[-2].astype(jnp.float32) ** 2 + rows[-1].astype(jnp.float32) ** 2
        ysq += left.astype(jnp.float32) ** 2 + right.astype(jnp.float32) ** 2
    rows = jnp.concatenate(rows, axis=1)
    columns = jnp.concatenate(columns, axis=1)
    total = lax.dot_general(rows, columns, LAST, preferred_element_type=jnp.float32)
    if not first:
        total += acc_ref[...]
    if last:
        xsq_column = jnp.sum(xsq, axis=1, keepdims=True)
        ysq_row = jnp.sum(ysq.T, axis=0, keepdims=True)
        total = (2.0 * total - xsq_column - ysq_row) * scale
        lanes = range(0, total.shape[1], half)
        top = functools.reduce(jnp.maximum, [total[:, k : k + half] for k in lanes])
        grown = jnp.exp(total - jnp.max(top, axis=1, keepdims=True))
        grown = functools.reduce(jnp.add, [grown[:, k : k + half] for k in lanes])
        refs[3][0:1, :] = jnp.max(top.T, axis=0, keepdims=True)
        refs[3][1:2, :] = jnp.sum(grown.T, axis=0, keepdims=True)
    else:
        refs[3][...] = xsq
        refs[4][...] = ysq
    out_ref[...] = total


def cost_step(words, pairs, chunks, start, carry, scale):
    size = len(chunks)
    last = start + size == Z
    block = start // size
    total, _, rows, half = pairs.shape
    columns, width = chunks[0].shape
    first = carry is None
    part = pl.BlockSpec((size, CORES, rows, half), lambda i, core, z: (block, 0, 0, 0))
    part_d = pl.BlockSpec((size, columns, half), lambda i, core, z: (block, 0, 0))
    tile = pl.BlockSpec((rows, columns), lambda i, core, z: (0, 0))
    narrow = pl.BlockSpec((rows, half), lambda i, core, z: (0, 0))
    whole = pl.BlockSpec(memory_space=pl.ANY)
    in_specs = [part] + [pl.BlockSpec((columns, width), lambda i, core, z: (0, 0))] * size
    args = [*words, pairs, *chunks]
    aliases = {}
    if not first:
        aliases = {len(args) + k: k for k in ((1, 2) if last else range(5))}
        in_specs += [tile, whole, whole, narrow, narrow]
        args += list(carry)
    halves = jax.ShapeDtypeStruct((total, columns, half), jnp.bfloat16)
    stats = pl.BlockSpec((2, rows), lambda i, core, z: (0, 0))
    sums = [jax.ShapeDtypeStruct((rows, half), jnp.float32)] * 2
    if last:
        sums = [jax.ShapeDtypeStruct((2, rows), jnp.float32)]
    return pl.pallas_call(
        functools.partial(cost_kernel, first=first, last=last, scale=scale),
        grid_spec=pltpu.PrefetchScalarGridSpec(
            num_scalar_prefetch=2, grid=(1,), in_specs=in_specs, out_specs=[tile, part_d, part_d] + ([stats] if last else [narrow] * 2)
        ),
        out_shape=[jax.ShapeDtypeStruct((rows, columns), jnp.float32), halves, halves, *sums],
        input_output_aliases=aliases,
        compiler_params=pltpu.CompilerParams(
            dimension_semantics=("arbitrary",), vmem_limit_bytes=COST_GRANTS[last]
        ),
        cost_estimate=pl.CostEstimate(
            flops=2 * rows * columns * width * size, bytes_accessed=6 * 1024 * 1024, transcendentals=0
        ),
        name="cost",
    )(*args)


def mix_kernel(core_ref, z_ref, own_w_ref, other_w_ref, own_d_ref, other_d_ref, out_ref, tail_ref):
    rows, columns = own_w_ref.shape
    count, half = out_ref.shape[0], out_ref.shape[2]
    step = pl.program_id(0)

    @pl.when(step == 0)
    def _():
        ones = jnp.ones((EXTRA, columns), jnp.bfloat16)
        left = lax.dot_general(ones, own_w_ref[...], LAST, preferred_element_type=jnp.float32)
        left += lax.dot_general(ones, other_w_ref[...], LAST, preferred_element_type=jnp.float32)
        line = lax.broadcasted_iota(jnp.int32, (EXTRA, half), 0)
        tail = jnp.zeros((EXTRA, half), jnp.float32)
        pieces = rows // half
        for part in range(3):
            rounded = left.astype(jnp.bfloat16).astype(jnp.float32)
            left = left - rounded
            for k in range(pieces):
                tail = jnp.where(
                    line == part * pieces + k, rounded[:, k * half : (k + 1) * half], tail
                )
        tail_ref[...] = tail.astype(jnp.bfloat16)

    slots = []
    for k in range(count):
        chunk = lax.rem(step * count + k - z_ref[0] + Z, Z)
        turned = lax.rem(Z - chunk, Z)
        pair = [jnp.where(at < Z // 2, 2 * at, 2 * (Z - at) - 1) for at in (chunk, turned)]
        first = core_ref[0] == 0
        slots.append((jnp.where(first, pair[0], pair[1]), jnp.where(first, pair[1], pair[0])))
    own_d = jnp.concatenate([own_d_ref[slot] for slot, _ in slots], axis=1)
    other_d = jnp.concatenate([other_d_ref[slot] for _, slot in slots], axis=1)
    plan = jnp.concatenate([own_w_ref[...], other_w_ref[...]], axis=1)
    total = jnp.dot(plan, jnp.concatenate([own_d, other_d], axis=0), preferred_element_type=jnp.float32)
    for k in range(count):
        out_ref[k, :rows, :] = total[:, k * half : (k + 1) * half].astype(jnp.bfloat16)
        out_ref[k, rows:, :] = tail_ref[...]


def mixed(words, own_w, other_w, own_d, other_d):
    steps, columns, half = other_d.shape
    rows = own_w.shape[0]
    count = 4
    tile = pl.BlockSpec((rows, columns), lambda k, core, z: (0, 0))
    whole = pl.BlockSpec((steps, columns, half), lambda k, core, z: (0, 0, 0))
    return pl.pallas_call(
        mix_kernel,
        grid_spec=pltpu.PrefetchScalarGridSpec(
            num_scalar_prefetch=2,
            grid=(steps // count,),
            in_specs=[tile, tile, whole, whole],
            out_specs=pl.BlockSpec((count, rows + EXTRA, half), lambda k, core, z: (k, 0, 0)),
            scratch_shapes=[pltpu.VMEM((EXTRA, half), jnp.bfloat16)],
        ),
        out_shape=jax.ShapeDtypeStruct((steps, rows + EXTRA, half), jnp.bfloat16),
        compiler_params=pltpu.CompilerParams(
            dimension_semantics=("arbitrary",), vmem_limit_bytes=MIX_GRANT
        ),
        name="mix",
    )(*words, own_w, other_w, own_d, other_d)


def shards(noise, data):
    n_row, n_col = lax.axis_size("row"), lax.axis_size("col")
    rows, half = noise.shape
    columns = data.shape[0]
    width = half * n_col
    core_word = jnp.full((1,), lax.rem(lax.axis_index("col"), CORES), jnp.int32)
    z_word = jnp.full((1,), lax.axis_index("row"), jnp.int32)
    pairs = lax.all_to_all(
        copied(noise, COLS), AXES, 0, 0, axis_index_groups=WHOLE
    ).reshape((CHIPS, CORES) + noise.shape)
    forth = back = data
    chunks = [data]
    for far in range(1, Z // 2 + 1):
        forth = lax.ppermute(forth, AXES, FORTH)
        chunks.append(forth)
        if far < Z // 2:
            back = lax.ppermute(back, AXES, BACK)
            chunks.append(back)
    carry = None

    def cost(call):
        start, size = CALLS[call]
        now = chunks[start : start + size]
        return cost_step((core_word, z_word), pairs, now, start, carry, 1.0 / (width * blur))

    for call in range(len(CALLS)):
        carry = cost(call)
    scores, own_d, sent, stats = carry
    other_d = lax.ppermute(sent, "col", SWAP)

    shift = math.log(rows * n_row / (columns * n_col))
    f = g = None
    for step in range(ITERS):
        if step == 0:
            pairs = gathered(stats, "col", n_col)
            top = jnp.max(pairs[:, 0], axis=0)
            f = -top - jnp.log(jnp.sum(pairs[:, 1] * jnp.exp(pairs[:, 0] - top), axis=0))
            shifted = scores + f[:, None]
            top = jnp.max(shifted, axis=0)
            total = jnp.sum(jnp.exp(shifted - top[None, :]), axis=0)
            pairs = gathered(jnp.stack([top, total]), "row", n_row)
            top = jnp.max(pairs[:, 0], axis=0)
            g = shift - top - jnp.log(jnp.sum(pairs[:, 1] * jnp.exp(pairs[:, 0] - top), axis=0))
        else:
            total = jnp.sum(jnp.exp(scores + f[:, None] + g[None, :]), axis=1)
            f = f - jnp.log(jnp.sum(gathered(total[None], "col", n_col), axis=(0, 1)))
            total = jnp.sum(jnp.exp(scores + f[:, None] + g[None, :]), axis=0)
            g = g + shift - jnp.log(jnp.sum(gathered(total[None], "row", n_row), axis=(0, 1)))

    own_w = jnp.exp(scores + f[:, None] + g[None, :]).astype(jnp.bfloat16)
    other_w = lax.ppermute(own_w, "col", SWAP)
    pieces = mixed((core_word, z_word), own_w, other_w, own_d, other_d)
    f, g, pieces = lax.optimization_barrier((f * blur, g * blur, pieces))
    landed = lax.all_to_all(pieces, "col", 0, 0, axis_index_groups=PLANE)
    summed = jnp.sum(landed.astype(jnp.float32), axis=0)
    mass = jnp.sum(summed[rows:].reshape(-1)[: 3 * rows].reshape(3, rows), axis=0)
    target = (summed[:rows] / mass[:, None] - noise.astype(jnp.float32)).astype(jnp.bfloat16)
    return (target, f, g)


def solution(mesh):
    return jax.shard_map(
        shards,
        mesh=mesh,
        in_specs=(P("row", "col"), P("col", "row")),
        out_specs=(P("row", "col"), P("row"), P("col")),
        check_vma=False,
    )
```

```python
import functools
import math

import jax
import jax.numpy as jnp
from jax import lax
from jax.experimental import pallas as pl
from jax.experimental.pallas import tpu as pltpu
from jax.sharding import PartitionSpec as P

ITERS = 4
blur = 0.01
X, Y, CORES, Z = 4, 4, 2, 16
CHIPS = X * Y
COLS = CHIPS * CORES
EXTRA = 16
CALLS = [(0, 14), (14, 2)]
COST_GRANTS = (48 * 1024 * 1024, 50 * 1024 * 1024)
MIX_GRANT = 28 * 1024 * 1024
AXES = ("row", "col")

ORDER = [0]
for far in range(1, Z // 2):
    ORDER += [Z - far, far]
ORDER.append(Z // 2)

PLANE = [[chip * CORES + core for chip in range(CHIPS)] for core in range(CORES)]
WHOLE = [
    [z * COLS + (z + k) % CHIPS * CORES + core for k in ORDER for core in range(CORES)] for z in range(Z)
]
SWAP = [(index, index ^ 1) for index in range(COLS)]
FORTH = [(z, (z + 1) % Z) for z in range(Z)]
BACK = [(z, (z - 1) % Z) for z in range(Z)]
LAST = (((1,), (1,)), ((), ()))


def gathered(value, axis, count):
    copies = jnp.broadcast_to(value[None], (count,) + value.shape)
    return lax.all_to_all(copies, axis, 0, 0)


def copies_kernel(value_ref, out_ref, done):
    copies = [pltpu.make_async_copy(value_ref, out_ref.at[k], done.at[k]) for k in range(out_ref.shape[0])]
    for copy in copies:
        copy.start()
    for copy in copies:
        copy.wait()


def copied(value, count):
    return pl.pallas_call(
        copies_kernel,
        in_specs=[pl.BlockSpec(memory_space=pltpu.VMEM)],
        out_specs=pl.BlockSpec(memory_space=pl.ANY),
        out_shape=jax.ShapeDtypeStruct((count,) + value.shape, value.dtype),
        scratch_shapes=[pltpu.SemaphoreType.DMA((count,))],
        name="copies",
    )(value)


def cost_kernel(core_ref, z_ref, noise_ref, *refs, first, last, scale):
    size = noise_ref.shape[0]
    data_refs, refs = refs[:size], refs[size:]
    if not first:
        acc_ref, x_acc_ref, y_acc_ref, refs = refs[0], refs[3], refs[4], refs[5:]
    out_ref, keep_ref, sent_ref = refs[:3]
    low = core_ref[0] == 0
    half = noise_ref.shape[3]
    rows, columns = [], []
    xsq = ysq = 0.0
    if not first:
        xsq, ysq = x_acc_ref[...], y_acc_ref[...]
    for k in range(size):
        rows += [noise_ref[k, 0], noise_ref[k, 1]]
        chunk = data_refs[k][...]
        columns.append(chunk)
        left, right = chunk[:, :half], chunk[:, half:]
        keep_ref[k] = jnp.where(low, left, right)
        sent_ref[k] = jnp.where(low, right, left)
        xsq += rows[-2].astype(jnp.float32) ** 2 + rows[-1].astype(jnp.float32) ** 2
        ysq += left.astype(jnp.float32) ** 2 + right.astype(jnp.float32) ** 2
    rows = jnp.concatenate(rows, axis=1)
    columns = jnp.concatenate(columns, axis=1)
    total = lax.dot_general(rows, columns, LAST, preferred_element_type=jnp.float32)
    if not first:
        total += acc_ref[...]
    if last:
        xsq_column = jnp.sum(xsq, axis=1, keepdims=True)
        ysq_row = jnp.sum(ysq.T, axis=0, keepdims=True)
        total = (2.0 * total - xsq_column - ysq_row) * scale
        lanes = range(0, total.shape[1], half)
        top = functools.reduce(jnp.maximum, [total[:, k : k + half] for k in lanes])
        grown = jnp.exp(total - jnp.max(top, axis=1, keepdims=True))
        grown = functools.reduce(jnp.add, [grown[:, k : k + half] for k in lanes])
        refs[3][0:1, :] = jnp.max(top.T, axis=0, keepdims=True)
        refs[3][1:2, :] = jnp.sum(grown.T, axis=0, keepdims=True)
    else:
        refs[3][...] = xsq
        refs[4][...] = ysq
    out_ref[...] = total


def cost_step(words, pairs, chunks, start, carry, scale):
    size = len(chunks)
    last = start + size == Z
    block = start // size
    total, _, rows, half = pairs.shape
    columns, width = chunks[0].shape
    first = carry is None
    part = pl.BlockSpec((size, CORES, rows, half), lambda i, core, z: (block, 0, 0, 0))
    part_d = pl.BlockSpec((size, columns, half), lambda i, core, z: (block, 0, 0))
    tile = pl.BlockSpec((rows, columns), lambda i, core, z: (0, 0))
    narrow = pl.BlockSpec((rows, half), lambda i, core, z: (0, 0))
    whole = pl.BlockSpec(memory_space=pl.ANY)
    in_specs = [part] + [pl.BlockSpec((columns, width), lambda i, core, z: (0, 0))] * size
    args = [*words, pairs, *chunks]
    aliases = {}
    if not first:
        aliases = {len(args) + k: k for k in ((1, 2) if last else range(5))}
        in_specs += [tile, whole, whole, narrow, narrow]
        args += list(carry)
    halves = jax.ShapeDtypeStruct((total, columns, half), jnp.bfloat16)
    stats = pl.BlockSpec((2, rows), lambda i, core, z: (0, 0))
    sums = [jax.ShapeDtypeStruct((rows, half), jnp.float32)] * 2
    if last:
        sums = [jax.ShapeDtypeStruct((2, rows), jnp.float32)]
    return pl.pallas_call(
        functools.partial(cost_kernel, first=first, last=last, scale=scale),
        grid_spec=pltpu.PrefetchScalarGridSpec(
            num_scalar_prefetch=2, grid=(1,), in_specs=in_specs, out_specs=[tile, part_d, part_d] + ([stats] if last else [narrow] * 2)
        ),
        out_shape=[jax.ShapeDtypeStruct((rows, columns), jnp.float32), halves, halves, *sums],
        input_output_aliases=aliases,
        compiler_params=pltpu.CompilerParams(
            dimension_semantics=("arbitrary",), vmem_limit_bytes=COST_GRANTS[last]
        ),
        cost_estimate=pl.CostEstimate(
            flops=2 * rows * columns * width * size, bytes_accessed=6 * 1024 * 1024, transcendentals=0
        ),
        name="cost",
    )(*args)


def mix_kernel(
    z_ref, own_w_ref, other_w_ref, own_d_ref, other_d_ref, f_ref, g_ref, out_ref, f_out_ref, g_out_ref, tail_ref
):
    rows, columns = own_w_ref.shape
    count, half = out_ref.shape[0], out_ref.shape[2]
    step = pl.program_id(0)

    @pl.when(step == 0)
    def _():
        f_out_ref[...] = f_ref[...] * blur
        g_out_ref[...] = g_ref[...] * blur
        ones = jnp.ones((EXTRA, columns), jnp.bfloat16)
        left = lax.dot_general(ones, own_w_ref[...], LAST, preferred_element_type=jnp.float32)
        left += lax.dot_general(ones, other_w_ref[...], LAST, preferred_element_type=jnp.float32)
        line = lax.broadcasted_iota(jnp.int32, (EXTRA, half), 0)
        tail = jnp.zeros((EXTRA, half), jnp.float32)
        pieces = rows // half
        for part in range(3):
            rounded = left.astype(jnp.bfloat16).astype(jnp.float32)
            left = left - rounded
            for k in range(pieces):
                tail = jnp.where(
                    line == part * pieces + k, rounded[:, k * half : (k + 1) * half], tail
                )
        tail_ref[...] = tail.astype(jnp.bfloat16)

    slots = []
    for k in range(count):
        chunk = lax.rem(step * count + k - z_ref[0] + Z, Z)
        slots.append(jnp.where(chunk < Z // 2, 2 * chunk, 2 * (Z - chunk) - 1))
    own_d = jnp.concatenate([own_d_ref[slot] for slot in slots], axis=1)
    other_d = jnp.concatenate([other_d_ref[slot] for slot in slots], axis=1)
    plan = jnp.concatenate([own_w_ref[...], other_w_ref[...]], axis=1)
    total = jnp.dot(plan, jnp.concatenate([own_d, other_d], axis=0), preferred_element_type=jnp.float32)
    for k in range(count):
        out_ref[k, :rows, :] = total[:, k * half : (k + 1) * half].astype(jnp.bfloat16)
        out_ref[k, rows:, :] = tail_ref[...]


def mixed(z, own_w, other_w, own_d, other_d, f, g):
    steps, columns, half = other_d.shape
    rows = own_w.shape[0]
    count = 4
    tile = pl.BlockSpec((rows, columns), lambda k, z: (0, 0))
    whole = pl.BlockSpec((steps, columns, half), lambda k, z: (0, 0, 0))
    line = pl.BlockSpec((1, rows), lambda k, z: (0, 0))
    return pl.pallas_call(
        mix_kernel,
        grid_spec=pltpu.PrefetchScalarGridSpec(
            num_scalar_prefetch=1,
            grid=(steps // count,),
            in_specs=[tile, tile, whole, whole, line, line],
            out_specs=[pl.BlockSpec((count, rows + EXTRA, half), lambda k, z: (k, 0, 0)), line, line],
            scratch_shapes=[pltpu.VMEM((EXTRA, half), jnp.bfloat16)],
        ),
        out_shape=[
            jax.ShapeDtypeStruct((steps, rows + EXTRA, half), jnp.bfloat16),
            jax.ShapeDtypeStruct((1, rows), jnp.float32),
            jax.ShapeDtypeStruct((1, columns), jnp.float32),
        ],
        compiler_params=pltpu.CompilerParams(
            dimension_semantics=("arbitrary",), vmem_limit_bytes=MIX_GRANT
        ),
        name="mix",
    )(z, own_w, other_w, own_d, other_d, f[None], g[None])


def shards(noise, data):
    n_row, n_col = lax.axis_size("row"), lax.axis_size("col")
    rows, half = noise.shape
    columns = data.shape[0]
    width = half * n_col
    core_word = jnp.full((1,), lax.rem(lax.axis_index("col"), CORES), jnp.int32)
    z_word = jnp.full((1,), lax.axis_index("row"), jnp.int32)
    pairs = lax.all_to_all(
        copied(noise, COLS), AXES, 0, 0, axis_index_groups=WHOLE
    ).reshape((CHIPS, CORES) + noise.shape)
    forth = back = data
    chunks = [data]
    for far in range(1, Z // 2 + 1):
        forth = lax.ppermute(forth, "row", FORTH)
        chunks.append(forth)
        if far < Z // 2:
            back = lax.ppermute(back, "row", BACK)
            chunks.append(back)
    carry = None

    def cost(call):
        start, size = CALLS[call]
        now = chunks[start : start + size]
        return cost_step((core_word, z_word), pairs, now, start, carry, 1.0 / (width * blur))

    for call in range(len(CALLS)):
        carry = cost(call)
    scores, own_d, sent, stats = carry
    other_d = lax.ppermute(sent, "col", SWAP)

    shift = math.log(rows * n_row / (columns * n_col))
    f = g = None
    for step in range(ITERS):
        if step == 0:
            pairs = gathered(stats, "col", n_col)
            top = jnp.max(pairs[:, 0], axis=0)
            f = -top - jnp.log(jnp.sum(pairs[:, 1] * jnp.exp(pairs[:, 0] - top), axis=0))
            shifted = scores + f[:, None]
            top = jnp.max(shifted, axis=0)
            total = jnp.sum(jnp.exp(shifted - top[None, :]), axis=0)
            pairs = gathered(jnp.stack([top, total]), "row", n_row)
            top = jnp.max(pairs[:, 0], axis=0)
            g = shift - top - jnp.log(jnp.sum(pairs[:, 1] * jnp.exp(pairs[:, 0] - top), axis=0))
        else:
            total = jnp.sum(jnp.exp(scores + f[:, None] + g[None, :]), axis=1)
            f = f - jnp.log(jnp.sum(gathered(total[None], "col", n_col), axis=(0, 1)))
            total = jnp.sum(jnp.exp(scores + f[:, None] + g[None, :]), axis=0)
            g = g + shift - jnp.log(jnp.sum(gathered(total[None], "row", n_row), axis=(0, 1)))

    own_w = jnp.exp(scores + f[:, None] + g[None, :]).astype(jnp.bfloat16)
    other_w = lax.ppermute(own_w, "col", SWAP)
    pieces, f, g = mixed(z_word, own_w, other_w, own_d, other_d, f, g)
    landed = lax.all_to_all(pieces, "col", 0, 0, axis_index_groups=PLANE)
    summed = jnp.sum(landed.astype(jnp.float32), axis=0)
    mass = jnp.sum(summed[rows:].reshape(-1)[: 3 * rows].reshape(3, rows), axis=0)
    target = (summed[:rows] / mass[:, None] - noise.astype(jnp.float32)).astype(jnp.bfloat16)
    return (target, f[0], g[0])


def solution(mesh):
    return jax.shard_map(
        shards,
        mesh=mesh,
        in_specs=(P("row", "col"), P("col", "row")),
        out_specs=(P("row", "col"), P("row"), P("col")),
        check_vma=False,
    )
```
